128 devices in a mesh: grp: 2 (over y_lo), dp: 8 (over x, y_hi), tensor: 8 (over z, core).
Axes of the slice: x: 4, y: 4 (y_hi: 2, y_lo: 2; y = y_hi * 2 + y_lo), z: 4, core: 2. Of those that a mesh axis runs over, the one named last changes fastest.
Arguments:
- teacher_values: bfloat16 [2048, 16384], P('grp', 'tensor'), may hold values from -6 to 6
- teacher_weight: bfloat16 [16384, 16384], P('tensor', 'dp'), may hold values from -0.046875 to 0.046875
- teacher_stream: bfloat16 [2048, 16384], P(('grp', 'tensor'), 'dp'), may hold values from -6 to 6
- send_order: int32 [16, 128], replicated, may hold values from 0 to 127, each once within a row
- projection: bfloat16 [16384, 8192], P('dp', 'tensor'), may hold values from -0.046875 to 0.046875
- student_values: bfloat16 [2048, 8192], P(('grp', 'tensor'), 'dp'), may hold values from -0.75 to 0.75
- student_weight: bfloat16 [8192, 8192], P('dp', 'tensor'), may hold values from -0.5 to 0.5
- student_stream: bfloat16 [2048, 8192], P(('grp', 'dp'), 'tensor'), may hold values from -6 to 6
Outputs:
- values_grad: float32 [2048, 8192], P(('grp', 'tensor'), 'dp')
- weight_grad: float32 [8192, 8192], P('dp', 'tensor')
The draws below stay inside these ranges and needn't reach their ends.
Inputs may be any that keep to these rules, and one draw needn't show every extreme that they name: `send_order`: each row is an ordering of the 128 rows of one teacher block.
All inputs are finite; a program needn't handle non-finite values.
Results may differ from the reference program's by a relative error of at most 0.0085.
Values may be sent and summed in bfloat16 or wider, within the bound.
No kernel may reach another device: no remote copies, remote signals or barrier semaphores. Data moves between devices by JAX's collectives and lax.ppermute only.
A program may use at most 128 MiB of HBM per device.

```python
import math
import jax
import jax.numpy as jnp
from jax import lax

DT = 16384
DS = 8192
TOK_DEV = 128
BLOCKS = 16
PIECE = 8
TOKENS = 2048


def strengthened(values, stream_key, source, target, parts, factor):
    def block_of(position):
        return (jnp.arange(values.shape[position]) // (values.shape[position] // parts)).reshape((-1,) + (1,) * (values.ndim - 1 - position))

    first = jax.random.permutation(stream_key, parts)[block_of(target)]
    far = (block_of(target) + parts // 2) % parts
    return jnp.where((block_of(source) == first) | (block_of(source) == far), factor * values, values)


def shard_levels(key, shape, split, least, high):
    gain = 1.0
    for position, shards_of in split:
        draws = jax.random.uniform(jax.random.fold_in(jax.random.fold_in(key, 6), position), (shards_of,), jnp.float32, least / len(split), high / len(split))
        gain = gain * jnp.repeat(jnp.exp(draws), shape[position] // shards_of).reshape((-1,) + (1,) * (len(shape) - 1 - position))
    return gain


def scatter_about(stream_key, shape, scale, reach, pieces=(), kind=jnp.bfloat16):
    gain = shard_levels(stream_key, shape, pieces, -0.22, 0.18) if pieces else 1.0
    drawn = jax.random.normal(stream_key, shape, jnp.float32) * scale * gain
    return jnp.minimum(jnp.maximum(drawn, -reach), reach).astype(kind)


def noise_with(rng, dims, spread, bound, cuts, heavy, kind=jnp.bfloat16):
    entries = spread * jax.random.normal(rng, dims, jnp.float32)
    if cuts:
        entries = entries * shard_levels(rng, dims, cuts, -0.22, 0.18)
    return jnp.clip(strengthened(entries, jax.random.fold_in(rng, 3), *heavy), -bound, bound).astype(kind)


def setup_inputs(seed: int = 0) -> dict:
    key_list = jax.random.split(jax.random.key(seed), 9)
    teacher_values = noise_with(key_list[0], (TOKENS, DT), 1.0, 6.0, ((0, 2), (1, 8)), (1, 0, 8, 2.0))
    teacher_weight = scatter_about(key_list[1], (DT, DT), DT ** -0.5, 0.046875, ((0, 8), (1, 8)))
    teacher_stream = scatter_about(key_list[2], (TOKENS, DT), 1.0, 6.0, ((0, 16), (1, 8)))
    send_order = jax.vmap(lambda own: jax.random.permutation(own, TOK_DEV))(jax.random.split(key_list[3], BLOCKS)).reshape((BLOCKS, TOK_DEV)).astype(jnp.int32)
    projection = scatter_about(key_list[4], (DT, DS), DT ** -0.5, 0.046875, ((0, 8), (1, 8)))
    student_values = noise_with(key_list[5], (TOKENS, DS), 0.125, 0.75, ((0, 16), (1, 8)), (1, 0, 16, 2.0))
    student_weight = scatter_about(key_list[6], (DS, DS), (DS // 64) ** -0.5, 0.5, ((0, 8), (1, 8)))
    student_stream = scatter_about(key_list[7], (TOKENS, DS), 1.0, 6.0, ((0, 16), (1, 8)))
    return dict(teacher_values=teacher_values, teacher_weight=teacher_weight, teacher_stream=teacher_stream, send_order=send_order, projection=projection, student_values=student_values, student_weight=student_weight, student_stream=student_stream)


def reference(teacher_values, teacher_weight, teacher_stream, send_order, projection, student_values, student_weight, student_stream):
    teacher_out = jnp.dot(teacher_values, teacher_weight, preferred_element_type=jnp.float32)
    hidden = (teacher_stream.astype(jnp.float32) + teacher_out).astype(jnp.bfloat16)
    base = (jnp.arange(BLOCKS, dtype=jnp.int32) * TOK_DEV)[:, None]
    source = (base + send_order.astype(jnp.int32)).reshape(BLOCKS, BLOCKS, PIECE)
    source = jnp.transpose(source, (1, 0, 2)).reshape(TOKENS)
    relayed = jnp.take(hidden, source, axis=0)
    target = jnp.dot(relayed, projection, preferred_element_type=jnp.float32).astype(jnp.bfloat16)
    layer_out = jnp.dot(student_values, student_weight, preferred_element_type=jnp.float32)
    loss_scale = 1.0 / math.sqrt(TOKENS)
    gap = ((student_stream.astype(jnp.float32) + layer_out - target.astype(jnp.float32)) * loss_scale).astype(jnp.bfloat16)
    values_grad = lax.dot_general(gap, student_weight, (((1,), (1,)), ((), ())), preferred_element_type=jnp.float32)
    weight_grad = lax.dot_general(student_values, gap, (((0,), (0,)), ((), ())), preferred_element_type=jnp.float32)
    return (values_grad, weight_grad)
```

```python
import functools
import math

import jax
import jax.numpy as jnp
from jax import lax
from jax.experimental import pallas as pl
from jax.experimental.pallas import tpu as pltpu
from jax.sharding import Mesh, PartitionSpec as P

BF16 = jnp.bfloat16
F32 = jnp.float32
CHUNKS = 2
X = "x"
Z = "z"
CORE = "core"
GRP = "grp"
DP = ("x", "yh")
Y = ("grp", "yh")
SIZES = {"grp": 2, "x": 4, "yh": 2, "z": 4, "core": 2}
VMEM_LIMIT = 56 * 1024 * 1024


def swap(array, axes, distance):
    names = axes if isinstance(axes, tuple) else (axes,)
    size = math.prod(SIZES[name] for name in names)
    return lax.ppermute(array, axes, [(i, i ^ distance) for i in range(size)])


def params():
    return pltpu.CompilerParams(vmem_limit_bytes=VMEM_LIMIT)


def cost(macs, moved):
    return pl.CostEstimate(flops=2 * macs, bytes_accessed=moved, transcendentals=0)


def whole(array):
    return pl.BlockSpec(array.shape, lambda *_: (0,) * array.ndim)


def smem():
    return pl.BlockSpec(memory_space=pltpu.SMEM)


def nn(a, b):
    return jnp.dot(a, b, preferred_element_type=F32)


def nt(a, b):
    return lax.dot_general(a, b, (((1,), (1,)), ((), ())), preferred_element_type=F32)


def teacher_kernel(row_ref, own_ref, x_ref, w_ref, s_ref, mine_ref, peer_ref, a_ref, o_ref):
    rows, depth = a_ref.shape

    @pl.when(pl.program_id(0) == 0)
    def _():
        source = lax.broadcasted_iota(jnp.int32, (rows, rows), 1)
        pick = jnp.where(source == row_ref[...], 1.0, 0.0).astype(BF16)
        wide = 512

        def step(i, _):
            columns = pl.ds(pl.multiple_of(i * wide, wide), wide)
            a_ref[:, columns] = nn(pick, x_ref[:, columns]).astype(BF16)
            return 0

        lax.fori_loop(0, depth // wide, step, 0)
        source = lax.broadcasted_iota(jnp.int32, o_ref.shape, 1)
        o_ref[...] = jnp.where(source == own_ref[...], 1.0, 0.0).astype(BF16)

    out = (nn(a_ref[...], w_ref[...]) + nn(o_ref[...], s_ref[...])).astype(BF16)
    mine_ref[...] = out[: rows // 2]
    peer_ref[...] = out[rows // 2 :]


def teacher(row, own, values, weight, stream, chunk, tile=256):
    rows, depth = values.shape[0] // CHUNKS, values.shape[1]
    width = weight.shape[1]
    half = jax.ShapeDtypeStruct((rows // 2, width), BF16)
    return pl.pallas_call(
        teacher_kernel,
        grid=(width // tile,),
        out_shape=(half, half),
        in_specs=[
            whole(row),
            whole(own),
            pl.BlockSpec((rows, depth), lambda j: (chunk, 0)),
            pl.BlockSpec((depth, tile), lambda j: (0, j)),
            pl.BlockSpec((stream.shape[0], tile), lambda j: (0, j)),
        ],
        out_specs=[pl.BlockSpec((rows // 2, tile), lambda j: (0, j))] * 2,
        scratch_shapes=[pltpu.VMEM((rows, depth), BF16), pltpu.VMEM((rows, stream.shape[0]), BF16)],
        compiler_params=params(),
        cost_estimate=cost(rows * depth * width, 2 * (depth * width + rows * depth + rows * width)),
    )(row, own, values, weight, stream)


def partial_kernel(ids_ref, *refs):
    hidden, values = refs[:8], refs[8:16]
    p_ref, w_ref = refs[16:18]
    outs = refs[18:26]
    h_ref, v_ref = refs[26:]
    piece = hidden[0].shape[0]

    @pl.when(pl.program_id(0) == 0)
    def _():
        for k in range(8):
            at = pl.multiple_of((ids_ref[0] ^ ids_ref[1] ^ k) * piece, piece)
            h_ref[pl.ds(at, piece), :] = hidden[k][...]
            v_ref[pl.ds(at, piece), :] = values[k][...]

    out = (nn(v_ref[...], w_ref[...]) - nn(h_ref[...], p_ref[...])).astype(BF16)
    for k in range(8):
        outs[k][...] = out[k * piece : (k + 1) * piece]


def partial_sums(ids, hidden, values, projection, weight, chunk, tile=256):
    piece, deep = hidden[0].shape
    depth, width = weight.shape
    rows = 8 * piece
    return pl.pallas_call(
        partial_kernel,
        grid=(width // tile,),
        out_shape=[jax.ShapeDtypeStruct((piece, width), BF16)] * 8,
        in_specs=[smem()]
        + [whole(hidden[0])] * 8
        + [pl.BlockSpec((piece, depth), lambda j: (chunk, 0))] * 8
        + [pl.BlockSpec((deep, tile), lambda j: (0, j)), pl.BlockSpec((depth, tile), lambda j: (0, j))],
        out_specs=[pl.BlockSpec((piece, tile), lambda j: (0, j))] * 8,
        scratch_shapes=[pltpu.VMEM((rows, deep), BF16), pltpu.VMEM((rows, depth), BF16)],
        compiler_params=params(),
        cost_estimate=cost(rows * (deep + depth) * width, 2 * (deep + depth) * (width + rows)),
    )(ids, *hidden, *values, projection, weight)


def gap_places(first, second):
    piece = first[0].shape[0] // 2
    for e in range(4):
        for n in range(2):
            yield 2 * e + n, 0, first[e], n * piece
            yield 2 * e + n, 1, second[n], e * piece


def values_kernel(ids_ref, a0, a1, a2, a3, b0, b1, w_ref, mine_ref, peer_ref, g_ref):
    piece = a0.shape[0] // 2
    rows = g_ref.shape[0]
    block = CHUNKS * piece

    @pl.when(pl.program_id(0) == 0)
    def _():
        for k, chunk, ref, start in gap_places((a0, a1, a2, a3), (b0, b1)):
            to = ids_ref[0] ^ ids_ref[1] ^ k
            at = pl.multiple_of((to & 1) * (rows // 2) + (to >> 1) * block + chunk * piece, piece)
            g_ref[pl.ds(at, piece), :] = ref[start : start + piece, :]

    out = nt(g_ref[...], w_ref[...]).astype(BF16)
    mine_ref[...] = out[: rows // 2]
    peer_ref[...] = out[rows // 2 :]


def values_partial(ids, gaps, weight, tile=256):
    piece, width = gaps[0].shape[0] // 2, gaps[0].shape[1]
    rows = 8 * CHUNKS * piece
    feats = weight.shape[0]
    half = jax.ShapeDtypeStruct((rows // 2, feats), BF16)
    return pl.pallas_call(
        values_kernel,
        grid=(feats // tile,),
        out_shape=(half, half),
        in_specs=[smem()] + [whole(g) for g in gaps] + [pl.BlockSpec((tile, width), lambda j: (j, 0))],
        out_specs=[pl.BlockSpec((rows // 2, tile), lambda j: (0, j))] * 2,
        scratch_shapes=[pltpu.VMEM((rows, width), BF16)],
        compiler_params=params(),
        cost_estimate=cost(rows * width * feats, 2 * (rows * width + feats * width + rows * feats)),
    )(ids, *gaps, weight)


def turn_kernel(ids_ref, *refs):
    own, other, out_ref = refs[:8], refs[8:10], refs[10]
    rows = own[0].shape[0]
    for k in range(8):
        block = ids_ref[1] ^ k
        at = pl.multiple_of(block * rows, rows)
        out_ref[:, pl.ds(at, rows)] = own[k][...].T
        at = pl.multiple_of((block + 8) * rows, rows)
        start = (k >> 1) * rows
        out_ref[:, pl.ds(at, rows)] = other[k & 1][start : start + rows, :].T


def turned(ids, own, other):
    rows, feats = own[0].shape
    return pl.pallas_call(
        turn_kernel,
        out_shape=jax.ShapeDtypeStruct((feats, 16 * rows), BF16),
        in_specs=[smem()] + [pl.BlockSpec(memory_space=pltpu.VMEM)] * 10,
        out_specs=pl.BlockSpec(memory_space=pltpu.VMEM),
        compiler_params=params(),
        cost_estimate=cost(0, 64 * rows * feats),
    )(ids, *own, *other)


def weight_kernel(ids_ref, *refs):
    own, other = refs[:6], refs[6:12]
    v_ref, out_ref, g_ref = refs[12:]
    piece = own[0].shape[0] // 2
    half = g_ref.shape[0] // 2
    block = CHUNKS * piece

    @pl.when(pl.program_id(0) == 0)
    def _():
        for side, gaps in enumerate((own, other)):
            for k, chunk, ref, start in gap_places(gaps[:4], gaps[4:]):
                place = (ids_ref[0] ^ k) * block + side * half + chunk * piece
                at = pl.multiple_of(place, piece)
                g_ref[pl.ds(at, piece), :] = ref[start : start + piece, :]

    out_ref[...] = nn(v_ref[...], g_ref[...])


def weight_sums(ids, own, other, values, tile=256):
    feats, rows = values.shape
    width = own[0].shape[1]
    return pl.pallas_call(
        weight_kernel,
        grid=(feats // tile,),
        out_shape=jax.ShapeDtypeStruct((feats, width), F32),
        in_specs=[smem()]
        + [whole(g) for g in (*own, *other)]
        + [pl.BlockSpec((tile, rows), lambda j: (j, 0))],
        out_specs=pl.BlockSpec((tile, width), lambda j: (j, 0)),
        scratch_shapes=[pltpu.VMEM((rows, width), BF16)],
        compiler_params=params(),
        cost_estimate=cost(rows * width * feats, 2 * (rows * width + feats * rows + 2 * width * feats)),
    )(ids, *own, *other, values)


def add(*terms):
    total = terms[0].astype(F32)
    for term in terms[1:]:
        total = total + term.astype(F32)
    return total


def gather_tensor(block):
    across = [block, swap(block, Z, 1), swap(block, Z, 2), swap(block, Z, 3)]
    out = []
    for piece in across:
        out += [piece, swap(piece, CORE, 1)]
    return out


def per_device(
    teacher_values,
    teacher_weight,
    teacher_stream,
    send_order,
    projection,
    student_values,
    student_weight,
    student_stream,
):
    g = lax.axis_index("grp")
    dp = lax.axis_index("x") * 2 + lax.axis_index("yh")
    t = lax.axis_index("z") * 2 + lax.axis_index("core")
    ids = jnp.stack([dp, t]).astype(jnp.int32)
    piece = send_order.shape[1] // 16
    span = 8 // CHUNKS

    def ordered(rows):
        parts = rows.reshape(2, CHUNKS, -1, rows.shape[1])
        parts = jnp.where(g == 0, parts, parts[::-1])
        return parts.transpose(1, 0, 2, 3).reshape(rows.shape)

    def unordered(rows):
        parts = rows.reshape(CHUNKS, 2, -1, rows.shape[1]).transpose(1, 0, 2, 3)
        return jnp.where(g == 0, parts, parts[::-1]).reshape(rows.shape)

    order = lax.dynamic_slice_in_dim(send_order, g * 8, 8, 0).reshape(8, 16, piece)
    place = jnp.arange(16)
    core_far, z_far, half_far = place // 8, (place // 2) % 4, place % 2
    owner = (half_far ^ g) * 8 + (t ^ (z_far * 2 + core_far))
    chosen = owner[:, None] == jnp.arange(16)[None, :]
    order = jnp.sum(jnp.where(chosen[None, :, :, None], order[:, None], 0), axis=2)
    block = jnp.arange(8)[:, None, None]
    rows_of = ((block % span) * (16 * piece) + order).reshape(CHUNKS, span, 16, piece)
    owns_of = jnp.where(block == t, order, -1).reshape(CHUNKS, span, 16, piece)
    rows_of = rows_of.transpose(0, 2, 1, 3).reshape(CHUNKS, -1, 1)
    owns_of = owns_of.transpose(0, 2, 1, 3).reshape(CHUNKS, -1, 1)

    values = ordered(student_values)
    stream = ordered(student_stream)
    values_own = gather_tensor(values)
    pair = jnp.concatenate(values_own[0::2], axis=0)
    values_far = swap(pair, GRP, 1)
    values_other = [values_far, swap(values_far, CORE, 1)]

    loss_scale = 1.0 / math.sqrt(student_stream.shape[0] * 16)
    gaps = []
    for chunk in range(CHUNKS):
        mine, peer = teacher(
            rows_of[chunk], owns_of[chunk], teacher_values, teacher_weight, teacher_stream, chunk
        )
        arrived = swap(peer, CORE, 1)
        rows = mine.shape[0] // 4
        sums = [
            add(mine[k * rows : (k + 1) * rows], arrived[k * rows : (k + 1) * rows]).astype(BF16)
            for k in range(4)
        ]
        hidden = add(sums[0], *[swap(sums[k], Z, k) for k in (1, 2, 3)]).astype(BF16)
        relayed = swap(hidden[rows // 2 :], GRP, 1)
        hidden = jnp.concatenate([hidden[: rows // 2], relayed], axis=0)
        parts = partial_sums(
            ids, gather_tensor(hidden), values_own, projection, student_weight, chunk
        )
        total = add(parts[0], *[swap(parts[k], DP, k) for k in range(1, 8)])
        rows = total.shape[0]
        gap = stream[chunk * rows : (chunk + 1) * rows].astype(F32) + total
        gaps.append((gap * loss_scale).astype(BF16))

    first, second = gaps
    near = jnp.concatenate([first, swap(first, Y, 1)], axis=0)
    far = jnp.concatenate([swap(first, Y, 2), swap(first, Y, 3)], axis=0)
    along = jnp.concatenate([second] + [swap(second, X, k) for k in (1, 2, 3)], axis=0)
    own = [near] + [swap(near, X, k) for k in (1, 2, 3)] + [along, swap(along, Y, 1)]
    other = [far] + [swap(far, X, k) for k in (1, 2, 3)] + [swap(along, Y, 2), swap(along, Y, 3)]

    mine, peer = values_partial(ids, own, student_weight)
    arrived = swap(peer, CORE, 1)
    rows = mine.shape[0] // 4
    sums = [
        add(mine[k * rows : (k + 1) * rows], arrived[k * rows : (k + 1) * rows]) for k in range(4)
    ]
    values_grad = add(sums[0], *[swap(sums[k].astype(BF16), Z, k) for k in (1, 2, 3)])
    weight_grad = weight_sums(ids, own, other, turned(ids, values_own, values_other))
    return (unordered(values_grad), weight_grad)


def solution(mesh):
    fine = Mesh(mesh.devices.reshape(2, 4, 2, 4, 2), ("grp", "x", "yh", "z", "core"))
    tensor = ("z", "core")
    in_specs = (
        P("grp", tensor),
        P(tensor, DP),
        P(("grp",) + tensor, DP),
        P(),
        P(DP, tensor),
        P(("grp",) + tensor, DP),
        P(DP, tensor),
        P(("grp",) + DP, tensor),
    )
    out_specs = (P(("grp",) + tensor, DP), P(DP, tensor))
    return jax.shard_map(
        per_device, mesh=fine, in_specs=in_specs, out_specs=out_specs, check_vma=False
    )
```

```python
import functools
import math

import jax
import jax.numpy as jnp
from jax import lax
from jax.experimental import pallas as pl
from jax.experimental.pallas import tpu as pltpu
from jax.sharding import Mesh, PartitionSpec as P

BF16 = jnp.bfloat16
F32 = jnp.float32
SPAN = 2
LONG = 50
SHORT = 0.01
X = "x"
Z = "z"
CORE = "core"
GRP = "grp"
DP = ("x", "yh")
Y = ("grp", "yh")
SIZES = {"grp": 2, "x": 4, "yh": 2, "z": 4, "core": 2}
VMEM_LIMIT = 62 * 1024 * 1024


def swap(array, axes, distance):
    names = axes if isinstance(axes, tuple) else (axes,)
    size = math.prod(SIZES[name] for name in names)
    return lax.ppermute(array, axes, [(i, i ^ distance) for i in range(size)])


def params():
    return pltpu.CompilerParams(vmem_limit_bytes=VMEM_LIMIT)


def call(micros, body, grid, out_shape, in_specs, out_specs, scratch, *args):
    return pl.pallas_call(
        body,
        grid=grid,
        out_shape=out_shape,
        in_specs=in_specs,
        out_specs=out_specs,
        scratch_shapes=scratch,
        compiler_params=params(),
        cost_estimate=pl.CostEstimate(
            flops=int(micros * 1e9), bytes_accessed=1024, transcendentals=0
        ),
    )(*args)


def whole(array):
    return pl.BlockSpec(array.shape, lambda *_: (0,) * array.ndim)


def smem():
    return pl.BlockSpec(memory_space=pltpu.SMEM)


def unread():
    return pl.BlockSpec(memory_space=pl.ANY)


def shape(rows, columns, kind=BF16):
    return jax.ShapeDtypeStruct((rows, columns), kind)


def nn(a, b):
    return jnp.dot(a, b, preferred_element_type=F32)


def nt(a, b):
    return lax.dot_general(a, b, (((1,), (1,)), ((), ())), preferred_element_type=F32)


def with_unread(body, count):
    return lambda *refs: body(*refs[count:])


def one_hot(hits):
    return jnp.where(hits, 1.0, 0.0).astype(BF16)


def pick_rows(piece, ids_ref, order_ref, x_ref, a_ref, o_ref, pick_ref):
    rows, size = pick_ref.shape[0], o_ref.shape[1]
    t, g = ids_ref[1], ids_ref[2]
    to = lax.broadcasted_iota(jnp.int32, (rows, rows), 0)
    at = lax.broadcasted_iota(jnp.int32, (rows, rows), 1)
    far = to // (piece * SPAN)
    owner = ((far % 2) ^ g) * 8 + (t ^ (((far // 2) % 4) * 2 + far // 8))
    wanted = one_hot(at == ((to // piece) % SPAN) * size + owner * piece + to % piece)
    line = lax.broadcasted_iota(jnp.int32, (size, size), 0)

    def part(k, _):
        for b in range(SPAN):
            order = order_ref[pl.ds(g * 8 + k * SPAN + b, 1), :]
            columns = slice(b * size, (b + 1) * size)
            pick_ref[:, columns] = nt(wanted[:, columns], one_hot(line == order)).astype(BF16)
        here = pl.ds(pl.multiple_of(k * rows, rows), rows)
        a_ref[here, :] = nn(pick_ref[...], x_ref[here, :]).astype(BF16)
        mine = t - k * SPAN
        inside = jnp.logical_and(mine >= 0, mine < SPAN).astype(F32)
        start = pl.multiple_of(jnp.clip(mine, 0, SPAN - 1) * size, size)
        o_ref[here, :] = (pick_ref[:, pl.ds(start, size)].astype(F32) * inside).astype(BF16)
        return 0

    lax.fori_loop(0, x_ref.shape[0] // rows, part, 0)


def teacher_tile(piece, a_ref, o_ref, w_ref, s_ref, mine_ref, peer_ref):
    group = piece * SPAN
    parts = a_ref.shape[0] // (16 * group)
    out = (nn(a_ref[...], w_ref[...]) + nn(o_ref[...], s_ref[...])).astype(BF16)
    for k in range(parts):
        for far in range(16):
            start = (k * 16 + far) * group
            to = ((far % 8) * parts + k) * group
            (mine_ref, peer_ref)[far // 8][to : to + group, :] = out[start : start + group]


def first_teacher_kernel(piece, ids_ref, order_ref, x_ref, w_ref, s_ref, *rest):
    mine_ref, peer_ref, a_ref, o_ref, pick_ref = rest

    @pl.when(pl.program_id(0) == 0)
    def _():
        pick_rows(piece, ids_ref, order_ref, x_ref, a_ref, o_ref, pick_ref)

    teacher_tile(piece, a_ref, o_ref, w_ref, s_ref, mine_ref, peer_ref)


def second_teacher_kernel(piece, a_ref, o_ref, w_ref, s_ref, mine_ref, peer_ref):
    teacher_tile(piece, a_ref, o_ref, w_ref, s_ref, mine_ref, peer_ref)


def first_teacher(ids, order, values, weight, stream, tile=512):
    rows, depth = values.shape
    width, size = weight.shape[1] // 2, stream.shape[0]
    piece = order.shape[1] // 16
    return call(
        LONG,
        functools.partial(first_teacher_kernel, piece),
        (width // tile,),
        [shape(rows // 2, width)] * 2 + [shape(rows, depth), shape(rows, size)],
        [
            smem(),
            whole(order),
            whole(values),
            pl.BlockSpec((depth, tile), lambda j: (0, j)),
            pl.BlockSpec((size, tile), lambda j: (0, j)),
        ],
        [pl.BlockSpec((rows // 2, tile), lambda j: (0, j))] * 2
        + [pl.BlockSpec((rows, depth), lambda j: (0, 0)), pl.BlockSpec((rows, size), lambda j: (0, 0))],
        [pltpu.VMEM((SPAN * size, SPAN * size), BF16)],
        ids,
        order,
        values,
        weight,
        stream,
    )


def second_teacher(picked, owned, weight, stream, piece, after, tile=512):
    rows, depth = picked.shape
    width, size = weight.shape[1] // 2, stream.shape[0]
    skip = width // tile
    return call(
        LONG,
        with_unread(functools.partial(second_teacher_kernel, piece), len(after)),
        (width // tile,),
        [shape(rows // 2, width)] * 2,
        [unread()] * len(after)
        + [
            whole(picked),
            whole(owned),
            pl.BlockSpec((depth, tile), lambda j: (0, j + skip)),
            pl.BlockSpec((size, tile), lambda j: (0, j + skip)),
        ],
        [pl.BlockSpec((rows // 2, tile), lambda j: (0, j))] * 2,
        [],
        *after,
        picked,
        owned,
        weight,
        stream,
    )


def merge_kernel(count, *refs):
    total = refs[0][...].astype(F32)
    for ref in refs[1:count]:
        total = total + ref[...].astype(F32)
    outs = refs[count:]
    rows = total.shape[0] // len(outs)
    for k, out in enumerate(outs):
        out[...] = total[k * rows : (k + 1) * rows].astype(BF16)


def merged(terms, pieces, after=(), micros=SHORT, steps=2):
    rows, width = terms[0].shape
    tile = width // steps
    return call(
        micros,
        with_unread(functools.partial(merge_kernel, len(terms)), len(after)),
        (steps,),
        [shape(rows // pieces, width)] * pieces,
        [unread()] * len(after) + [pl.BlockSpec((rows, tile), lambda j: (0, j))] * len(terms),
        [pl.BlockSpec((rows // pieces, tile), lambda j: (0, j))] * pieces,
        [],
        *after,
        *terms,
    )


def layer_kernel(ids_ref, near_ref, pair_ref, w_ref, out_ref, v_ref):
    block = v_ref.shape[0] // 8

    @pl.when(pl.program_id(0) == 0)
    def _():
        for k in range(8):
            place = (ids_ref[1] ^ k) * block
            ref = (near_ref, pair_ref)[k & 1]
            start = (k >> 1) * block
            v_ref[pl.ds(pl.multiple_of(place, block), block), :] = ref[start : start + block, :]

    out_ref[...] = nn(v_ref[...], w_ref[...])


def layer(ids, near, pair, weight, after, tile=512):
    rows = 2 * near.shape[0]
    depth, width = weight.shape
    return call(
        LONG,
        with_unread(layer_kernel, len(after)),
        (width // tile,),
        shape(rows, width, F32),
        [unread()] * len(after)
        + [smem(), whole(near), whole(pair), pl.BlockSpec((depth, tile), lambda j: (0, j))],
        pl.BlockSpec((rows, tile), lambda j: (0, j)),
        [pltpu.VMEM((rows, depth), BF16)],
        *after,
        ids,
        near,
        pair,
        weight,
    )


def target_kernel(ids_ref, *refs):
    hidden = refs[:6]
    l_ref, p_ref = refs[6:8]
    outs, h_ref = refs[8:-1], refs[-1]
    piece = hidden[0].shape[0]
    blocks = [(0, 0, 0), (2, 1, 0), (6, 2, 0), (4, 3, 0), (1, 4, 0), (3, 5, 0), (7, 5, 1), (5, 5, 2)]

    @pl.when(pl.program_id(0) == 0)
    def _():
        for far, k, start in blocks:
            at = pl.multiple_of((ids_ref[1] ^ far) * piece, piece)
            h_ref[pl.ds(at, piece), :] = hidden[k][start * piece : (start + 1) * piece, :]

    out = l_ref[...] - nn(h_ref[...], p_ref[...])
    rows = out.shape[0] // len(outs)
    for k, to in enumerate(outs):
        to[...] = out[k * rows : (k + 1) * rows].astype(to.dtype)


def less_target(ids, hidden, left, projection, half, outs, kind, after=(), tile=512):
    piece, deep = hidden[0].shape
    width = projection.shape[1]
    rows = 8 * piece
    return call(
        LONG,
        with_unread(target_kernel, len(after)),
        (width // tile,),
        [shape(rows // outs, width, kind)] * outs,
        [unread()] * len(after)
        + [smem()]
        + [whole(h) for h in hidden]
        + [pl.BlockSpec((rows, tile), lambda j: (0, j)), pl.BlockSpec((deep, tile), lambda j: (half, j))],
        [pl.BlockSpec((rows // outs, tile), lambda j: (0, j))] * outs,
        [pltpu.VMEM((rows, deep), BF16)],
        *after,
        ids,
        *hidden,
        left,
        projection,
    )


def gap_places(gaps, halves):
    piece = gaps[0].shape[0] // 4
    for half in range(halves):
        for e in range(4):
            for n in range(2):
                yield 2 * e + n, half, 0, gaps[e], (2 * half + n) * piece
                yield 2 * e + n, half, 1, gaps[4 + 2 * half + n], e * piece


def values_kernel(ids_ref, *refs):
    gaps = refs[:8]
    w_ref, mine_ref, peer_ref, g_ref = refs[8:]
    piece = gaps[0].shape[0] // 4
    rows = g_ref.shape[0]

    @pl.when(pl.program_id(0) == 0)
    def _():
        for k, _, part, ref, start in gap_places(gaps, 1):
            to = ids_ref[0] ^ ids_ref[1] ^ k
            place = (to & 1) * (rows // 2) + (to >> 1) * (2 * piece) + part * piece
            g_ref[pl.ds(pl.multiple_of(place, piece), piece), :] = ref[start : start + piece, :]

    out = nt(g_ref[...], w_ref[...]).astype(BF16)
    mine_ref[...] = out[: rows // 2]
    peer_ref[...] = out[rows // 2 :]


def values_partial(ids, gaps, weight, after, tile=512):
    rows, width = 4 * gaps[0].shape[0], gaps[0].shape[1]
    feats = weight.shape[0]
    return call(
        LONG,
        with_unread(values_kernel, len(after)),
        (feats // tile,),
        [shape(rows // 2, feats)] * 2,
        [unread()] * len(after)
        + [smem()]
        + [whole(g) for g in gaps]
        + [pl.BlockSpec((tile, width), lambda j: (j, 0))],
        [pl.BlockSpec((rows // 2, tile), lambda j: (0, j))] * 2,
        [pltpu.VMEM((rows, width), BF16)],
        *after,
        ids,
        *gaps,
        weight,
    )


def turn_kernel(ids_ref, near_ref, pair_ref, far_ref, far_pair_ref, out_ref):
    rows = near_ref.shape[0] // 4
    for half, refs in enumerate(((near_ref, pair_ref), (far_ref, far_pair_ref))):
        for flip, ref in enumerate(refs):
            for z in range(4):
                block = half * 8 + (ids_ref[1] ^ (z * 2 + flip))
                at = pl.multiple_of(block * rows, rows)
                out_ref[:, pl.ds(at, rows)] = ref[z * rows : (z + 1) * rows, :].T


def turned(ids, near, pair, far, far_pair, after):
    rows, feats = near.shape
    return call(
        LONG,
        with_unread(turn_kernel, len(after)),
        (1,),
        shape(feats, 4 * rows),
        [unread()] * len(after) + [smem()] + [whole(near)] * 4,
        pl.BlockSpec((feats, 4 * rows), lambda j: (0, 0)),
        [],
        *after,
        ids,
        near,
        pair,
        far,
        far_pair,
    )


def weight_kernel(ids_ref, *refs):
    gaps = refs[:8]
    v_ref, out_ref, g_ref = refs[8:]
    piece = gaps[0].shape[0] // 4

    @pl.when(pl.program_id(0) == 0)
    def _():
        for k, half, part, ref, start in gap_places(gaps, 2):
            place = half * (g_ref.shape[0] // 2) + (ids_ref[0] ^ k) * (2 * piece) + part * piece
            g_ref[pl.ds(pl.multiple_of(place, piece), piece), :] = ref[start : start + piece, :]

    out_ref[...] = nn(v_ref[...], g_ref[...])


def weight_sums(ids, gaps, values, after, tile=512):
    feats, rows = values.shape
    width = gaps[0].shape[1]
    return call(
        LONG,
        with_unread(weight_kernel, len(after)),
        (feats // tile,),
        shape(feats, width, F32),
        [unread()] * len(after)
        + [smem()]
        + [whole(g) for g in gaps]
        + [pl.BlockSpec((tile, rows), lambda j: (j, 0))],
        pl.BlockSpec((tile, width), lambda j: (j, 0)),
        [pltpu.VMEM((rows, width), BF16)],
        *after,
        ids,
        *gaps,
        values,
    )


def add(*terms):
    total = terms[0].astype(F32)
    for term in terms[1:]:
        total = total + term.astype(F32)
    return total


def join_kernel(*refs):
    rows = refs[0].shape[0]
    for k, ref in enumerate(refs[:-1]):
        refs[-1][k * rows : (k + 1) * rows, :] = ref[...]


def joined(arrays, after=(), micros=LONG):
    rows, width = arrays[0].shape
    tile = width // 2
    return call(
        micros,
        with_unread(join_kernel, len(after)),
        (2,),
        shape(rows * len(arrays), width),
        [unread()] * len(after) + [pl.BlockSpec((rows, tile), lambda j: (0, j))] * len(arrays),
        pl.BlockSpec((rows * len(arrays), tile), lambda j: (0, j)),
        [],
        *after,
        *arrays,
    )


def place_kernel(ids_ref, keep_ref, come_ref, out_ref):
    rows = keep_ref.shape[0]
    for away, ref in enumerate((keep_ref, come_ref)):
        out_ref[pl.ds(pl.multiple_of((ids_ref[2] ^ away) * rows, rows), rows), :] = ref[...]


def placed(ids, keep, come, after=(), micros=LONG):
    rows, width = keep.shape
    return call(
        micros,
        with_unread(place_kernel, len(after)),
        (1,),
        shape(2 * rows, width),
        [unread()] * len(after) + [smem(), whole(keep), whole(come)],
        pl.BlockSpec((2 * rows, width), lambda j: (0, 0)),
        [],
        *after,
        ids,
        keep,
        come,
    )


def marker_kernel(*refs):
    refs[-1][...] = jnp.zeros(refs[-1].shape, F32)


def marker(*after):
    return call(
        LONG,
        marker_kernel,
        (1,),
        shape(8, 128, F32),
        [unread()] * len(after),
        pl.BlockSpec((8, 128), lambda j: (0, 0)),
        [],
        *after,
    )


def gather_tensor(block, after=()):
    across = [swap(block, Z, k) for k in (1, 3, 2)]
    pair = swap(joined(across, after), CORE, 1)
    return [block, *across, swap(block, CORE, 1), pair]


def per_device(
    teacher_values,
    teacher_weight,
    teacher_stream,
    send_order,
    projection,
    student_values,
    student_weight,
    student_stream,
):
    g = lax.axis_index("grp")
    dp = lax.axis_index("x") * 2 + lax.axis_index("yh")
    t = lax.axis_index("z") * 2 + lax.axis_index("core")
    ids = jnp.stack([dp, t, g]).astype(jnp.int32)

    piece = send_order.shape[1] // 16

    loss_scale = 1.0 / math.sqrt(student_stream.shape[0] * 16)

    across = [swap(student_values, Z, k) for k in (1, 3, 2)]
    mine, peer, picked, owned = first_teacher(
        ids, send_order, teacher_values, teacher_weight, teacher_stream
    )
    near = joined((student_values, across[0], across[2], across[1]))
    early = merged((mine, swap(peer, CORE, 1)), 4, (near,))
    moved = [swap(early[k], Z, k) for k in (1, 3, 2)]
    mine, peer = second_teacher(
        picked, owned, teacher_weight, teacher_stream, piece, (early[0],)
    )
    keep, give = merged((early[0], *moved), 2, (mine,), LONG)
    late = merged((mine, swap(peer, CORE, 1)), 4, (keep,))
    moved = [swap(late[k], Z, k) for k in (1, 3, 2)]
    first = placed(ids, keep, swap(give, GRP, 1), (late[0],), SHORT)
    pair = swap(near, CORE, 1)
    far = swap(near, GRP, 1)
    layer_out = layer(ids, near, pair, student_weight, (first,))
    keep, give = merged((late[0], *moved), 2, (layer_out,), LONG)
    first = gather_tensor(first, (give, far))
    second = placed(ids, keep, swap(give, GRP, 1))
    left = less_target(ids, first, layer_out, projection, 0, 1, F32, (second,))[0]
    second = gather_tensor(second, (left,))
    parts = less_target(ids, second, left, projection, 1, 1, BF16)[0]

    parts = lax.all_to_all(parts.reshape(8, -1, parts.shape[1]), DP, 0, 0, tiled=True)
    total = student_stream.astype(F32) + jnp.sum(parts.astype(F32), axis=0)
    gap = (total * loss_scale).astype(BF16)

    rows = gap.shape[0] // 2
    first, second = gap[:rows], gap[rows:]
    around = joined([first] + [swap(first, Y, k) for k in (1, 2, 3)])
    along = joined([second] + [swap(second, X, k) for k in (1, 2, 3)])
    turn = turned(ids, near, pair, far, swap(far, CORE, 1), (around, along))
    gaps = [around] + [swap(around, X, k) for k in (1, 2, 3)]
    gaps += [along] + [swap(along, Y, k) for k in (1, 2, 3)]

    mine, peer = values_partial(ids, gaps, student_weight, (turn,))
    parts = merged((mine, swap(peer, CORE, 1)), 4, (marker(mine),))
    values_grad = add(parts[0], *[swap(parts[k], Z, k) for k in (1, 3, 2)])
    weight_grad = weight_sums(ids, gaps, turn, (parts[0],))
    return (values_grad, weight_grad)


def solution(mesh):
    fine = Mesh(mesh.devices.reshape(2, 4, 2, 4, 2), ("grp", "x", "yh", "z", "core"))
    tensor = ("z", "core")
    in_specs = (
        P("grp", tensor),
        P(tensor, DP),
        P(("grp",) + tensor, DP),
        P(),
        P(DP, tensor),
        P(("grp",) + tensor, DP),
        P(DP, tensor),
        P(("grp",) + DP, tensor),
    )
    out_specs = (P(("grp",) + tensor, DP), P(DP, tensor))
    return jax.shard_map(
        per_device, mesh=fine, in_specs=in_specs, out_specs=out_specs, check_vma=False
    )
```

```python
import functools
import math

import jax
import jax.numpy as jnp
from jax import lax
from jax.experimental import pallas as pl
from jax.experimental.pallas import tpu as pltpu
from jax.sharding import Mesh, PartitionSpec as P

BF16 = jnp.bfloat16
F32 = jnp.float32
SPAN = 2
LONG = 50
SHORT = 0.01
X = "x"
Z = "z"
CORE = "core"
GRP = "grp"
DP = ("x", "yh")
Y = ("grp", "yh")
SIZES = {"grp": 2, "x": 4, "yh": 2, "z": 4, "core": 2}
VMEM_LIMIT = 62 * 1024 * 1024


def swap(array, axes, distance):
    names = axes if isinstance(axes, tuple) else (axes,)
    size = math.prod(SIZES[name] for name in names)
    return lax.ppermute(array, axes, [(i, i ^ distance) for i in range(size)])


def params():
    return pltpu.CompilerParams(vmem_limit_bytes=VMEM_LIMIT)


def call(micros, body, grid, out_shape, in_specs, out_specs, scratch, *args):
    return pl.pallas_call(
        body,
        grid=grid,
        out_shape=out_shape,
        in_specs=in_specs,
        out_specs=out_specs,
        scratch_shapes=scratch,
        compiler_params=params(),
        cost_estimate=pl.CostEstimate(
            flops=int(micros * 1e9), bytes_accessed=1024, transcendentals=0
        ),
    )(*args)


def whole(array):
    return pl.BlockSpec(array.shape, lambda *_: (0,) * array.ndim)


def smem():
    return pl.BlockSpec(memory_space=pltpu.SMEM)


def unread():
    return pl.BlockSpec(memory_space=pl.ANY)


def shape(rows, columns, kind=BF16):
    return jax.ShapeDtypeStruct((rows, columns), kind)


def nn(a, b):
    return jnp.dot(a, b, preferred_element_type=F32)


def nt(a, b):
    return lax.dot_general(a, b, (((1,), (1,)), ((), ())), preferred_element_type=F32)


def with_unread(body, count):
    return lambda *refs: body(*refs[count:])


def one_hot(hits):
    return jnp.where(hits, 1.0, 0.0).astype(BF16)


def teacher_kernel(piece, ids_ref, order_ref, x_ref, w_ref, s_ref, mine_ref, peer_ref, pick_ref, out_ref):
    parts, rows = pick_ref.shape[:2]
    size = s_ref.shape[0]
    group = piece * SPAN
    t, g = ids_ref[1], ids_ref[2]

    @pl.when(pl.program_id(0) == 0)
    def _():
        to = lax.broadcasted_iota(jnp.int32, (rows, rows), 0)
        at = lax.broadcasted_iota(jnp.int32, (rows, rows), 1)
        far = to // group
        owner = ((far % 2) ^ g) * 8 + (t ^ (((far // 2) % 4) * 2 + far // 8))
        wanted = one_hot(at == ((to // piece) % SPAN) * size + owner * piece + to % piece)
        line = lax.broadcasted_iota(jnp.int32, (size, size), 0)
        for k in range(parts):
            for b in range(SPAN):
                order = order_ref[pl.ds(g * 8 + k * SPAN + b, 1), :]
                columns = slice(b * size, (b + 1) * size)
                pick_ref[k, :, columns] = nt(wanted[:, columns], one_hot(line == order)).astype(BF16)

    out_ref[...] = nn(x_ref[...], w_ref[...])
    own = pl.ds(pl.multiple_of(t * size, size), size)
    out_ref[own, :] = out_ref[own, :] + s_ref[...].astype(F32)
    for k in range(parts):
        part = out_ref[k * rows : (k + 1) * rows, :].astype(BF16)
        part = nn(pick_ref[k], part).astype(BF16)
        for far in range(16):
            to = ((far % 8) * parts + k) * group
            (mine_ref, peer_ref)[far // 8][to : to + group, :] = part[far * group : (far + 1) * group]


def teacher(ids, order, values, weight, stream, half, after=(), tile=512):
    rows, depth = values.shape
    width, size = weight.shape[1] // 2, stream.shape[0]
    skip = half * (width // tile)
    side = SPAN * size
    return call(
        LONG,
        with_unread(functools.partial(teacher_kernel, order.shape[1] // 16), len(after)),
        (width // tile,),
        [shape(rows // 2, width)] * 2,
        [unread()] * len(after)
        + [
            smem(),
            whole(order),
            whole(values),
            pl.BlockSpec((depth, tile), lambda j: (0, j + skip)),
            pl.BlockSpec((size, tile), lambda j: (0, j + skip)),
        ],
        [pl.BlockSpec((rows // 2, tile), lambda j: (0, j))] * 2,
        [pltpu.VMEM((rows // side, side, side), BF16), pltpu.VMEM((rows, tile), F32)],
        *after,
        ids,
        order,
        values,
        weight,
        stream,
    )


def merge_kernel(count, *refs):
    total = refs[0][...].astype(F32)
    for ref in refs[1:count]:
        total = total + ref[...].astype(F32)
    outs = refs[count:]
    rows = total.shape[0] // len(outs)
    for k, out in enumerate(outs):
        out[...] = total[k * rows : (k + 1) * rows].astype(BF16)


def merged(terms, pieces, after=(), micros=SHORT, steps=2):
    rows, width = terms[0].shape
    tile = width // steps
    return call(
        micros,
        with_unread(functools.partial(merge_kernel, len(terms)), len(after)),
        (steps,),
        [shape(rows // pieces, width)] * pieces,
        [unread()] * len(after) + [pl.BlockSpec((rows, tile), lambda j: (0, j))] * len(terms),
        [pl.BlockSpec((rows // pieces, tile), lambda j: (0, j))] * pieces,
        [],
        *after,
        *terms,
    )


def layer_kernel(ids_ref, near_ref, pair_ref, w_ref, out_ref, v_ref):
    block = v_ref.shape[0] // 8

    @pl.when(pl.program_id(0) == 0)
    def _():
        for k in range(8):
            place = (ids_ref[1] ^ k) * block
            ref = (near_ref, pair_ref)[k & 1]
            start = (k >> 1) * block
            v_ref[pl.ds(pl.multiple_of(place, block), block), :] = ref[start : start + block, :]

    out_ref[...] = nn(v_ref[...], w_ref[...]).astype(BF16)


def layer(ids, near, pair, weight, after, tile=512):
    rows = 2 * near.shape[0]
    depth, width = weight.shape
    return call(
        LONG,
        with_unread(layer_kernel, len(after)),
        (width // tile,),
        shape(rows, width),
        [unread()] * len(after)
        + [smem(), whole(near), whole(pair), pl.BlockSpec((depth, tile), lambda j: (0, j))],
        pl.BlockSpec((rows, tile), lambda j: (0, j)),
        [pltpu.VMEM((rows, depth), BF16)],
        *after,
        ids,
        near,
        pair,
        weight,
    )


def target_kernel(places, ids_ref, *refs):
    count = 1 + max(k for _, k, _ in places)
    hidden = refs[:count]
    l_ref, p_ref, out_ref, h_ref = refs[count:]
    piece = hidden[0].shape[0]

    @pl.when(pl.program_id(0) == 0)
    def _():
        for far, k, start in places:
            at = pl.multiple_of((ids_ref[1] ^ far) * piece, piece)
            h_ref[pl.ds(at, piece), :] = hidden[k][start * piece : (start + 1) * piece, :]

    out_ref[...] = (l_ref[...].astype(F32) - nn(h_ref[...], p_ref[...])).astype(BF16)


def less_target(ids, hidden, left, projection, half, after=(), tile=512):
    arrays, places = hidden
    piece, deep = arrays[0].shape
    rows, width = left.shape
    return call(
        LONG,
        with_unread(functools.partial(target_kernel, places), len(after)),
        (width // tile,),
        shape(rows, width),
        [unread()] * len(after)
        + [smem()]
        + [whole(h) for h in arrays]
        + [pl.BlockSpec((rows, tile), lambda j: (0, j)), pl.BlockSpec((deep, tile), lambda j: (half, j))],
        pl.BlockSpec((rows, tile), lambda j: (0, j)),
        [pltpu.VMEM((rows, deep), BF16)],
        *after,
        ids,
        *arrays,
        left,
        projection,
    )


def gap_places(gaps, halves):
    piece = gaps[0].shape[0] // 4
    for half in range(halves):
        for n in range(2):
            by_x = ((0, 0), (1, 0), (2 + half, 0), (4, 0))
            for e, (array, _) in enumerate(by_x):
                start = n if e == 2 else 2 * half + n
                yield 2 * e + n, half, 0, gaps[array], start * piece
            for e in range(4):
                if (half, n) == (0, 1):
                    array, start = 6 + e // 2, e % 2
                else:
                    array, start = {(0, 0): 5, (1, 0): 8, (1, 1): 9}[half, n], e
                yield 2 * e + n, half, 1, gaps[array], start * piece


def values_kernel(ids_ref, *refs):
    gaps = refs[:10]
    w_ref, mine_ref, peer_ref, g_ref = refs[10:]
    piece = gaps[0].shape[0] // 4
    rows = g_ref.shape[0]

    @pl.when(pl.program_id(0) == 0)
    def _():
        for k, _, part, ref, start in gap_places(gaps, 1):
            to = ids_ref[0] ^ ids_ref[1] ^ k
            place = (to & 1) * (rows // 2) + (to >> 1) * (2 * piece) + part * piece
            g_ref[pl.ds(pl.multiple_of(place, piece), piece), :] = ref[start : start + piece, :]

    out = nt(g_ref[...], w_ref[...]).astype(BF16)
    mine_ref[...] = out[: rows // 2]
    peer_ref[...] = out[rows // 2 :]


def values_partial(ids, gaps, weight, after, tile=512):
    rows, width = 4 * gaps[0].shape[0], gaps[0].shape[1]
    feats = weight.shape[0]
    return call(
        LONG,
        with_unread(values_kernel, len(after)),
        (feats // tile,),
        [shape(rows // 2, feats)] * 2,
        [unread()] * len(after)
        + [smem()]
        + [whole(g) for g in gaps]
        + [pl.BlockSpec((tile, width), lambda j: (j, 0))],
        [pl.BlockSpec((rows // 2, tile), lambda j: (0, j))] * 2,
        [pltpu.VMEM((rows, width), BF16)],
        *after,
        ids,
        *gaps,
        weight,
    )


def turn_kernel(ids_ref, near_ref, pair_ref, far_ref, far_pair_ref, out_ref):
    rows = near_ref.shape[0] // 4
    for half, refs in enumerate(((near_ref, pair_ref), (far_ref, far_pair_ref))):
        for flip, ref in enumerate(refs):
            for z in range(4):
                block = half * 8 + (ids_ref[1] ^ (z * 2 + flip))
                at = pl.multiple_of(block * rows, rows)
                out_ref[:, pl.ds(at, rows)] = ref[z * rows : (z + 1) * rows, :].T


def turned(ids, near, pair, far, far_pair, after):
    rows, feats = near.shape
    return call(
        LONG,
        with_unread(turn_kernel, len(after)),
        (1,),
        shape(feats, 4 * rows),
        [unread()] * len(after) + [smem()] + [whole(near)] * 4,
        pl.BlockSpec((feats, 4 * rows), lambda j: (0, 0)),
        [],
        *after,
        ids,
        near,
        pair,
        far,
        far_pair,
    )


def weight_kernel(ids_ref, *refs):
    gaps = refs[:10]
    v_ref, out_ref, g_ref = refs[10:]
    piece = gaps[0].shape[0] // 4

    @pl.when(pl.program_id(0) == 0)
    def _():
        for k, half, part, ref, start in gap_places(gaps, 2):
            place = half * (g_ref.shape[0] // 2) + (ids_ref[0] ^ k) * (2 * piece) + part * piece
            g_ref[pl.ds(pl.multiple_of(place, piece), piece), :] = ref[start : start + piece, :]

    out_ref[...] = nn(v_ref[...], g_ref[...])


def weight_sums(ids, gaps, values, after, tile=512):
    feats, rows = values.shape
    width = gaps[0].shape[1]
    return call(
        LONG,
        with_unread(weight_kernel, len(after)),
        (feats // tile,),
        shape(feats, width, F32),
        [unread()] * len(after)
        + [smem()]
        + [whole(g) for g in gaps]
        + [pl.BlockSpec((tile, rows), lambda j: (j, 0))],
        pl.BlockSpec((tile, width), lambda j: (j, 0)),
        [pltpu.VMEM((rows, width), BF16)],
        *after,
        ids,
        *gaps,
        values,
    )


def add(*terms):
    total = terms[0].astype(F32)
    for term in terms[1:]:
        total = total + term.astype(F32)
    return total


def join_kernel(*refs):
    start = 0
    for ref in refs[:-1]:
        refs[-1][start : start + ref.shape[0], :] = ref[...]
        start += ref.shape[0]


def joined(arrays, after=(), micros=LONG):
    rows, width = sum(array.shape[0] for array in arrays), arrays[0].shape[1]
    tile = width // 2
    return call(
        micros,
        with_unread(join_kernel, len(after)),
        (2,),
        shape(rows, width),
        [unread()] * len(after)
        + [pl.BlockSpec((array.shape[0], tile), lambda j: (0, j)) for array in arrays],
        pl.BlockSpec((rows, tile), lambda j: (0, j)),
        [],
        *after,
        *arrays,
    )


def place_kernel(ids_ref, keep_ref, come_ref, out_ref):
    rows = keep_ref.shape[0]
    for away, ref in enumerate((keep_ref, come_ref)):
        out_ref[pl.ds(pl.multiple_of((ids_ref[2] ^ away) * rows, rows), rows), :] = ref[...]


def placed(ids, keep, come, after=(), micros=LONG):
    rows, width = keep.shape
    return call(
        micros,
        with_unread(place_kernel, len(after)),
        (1,),
        shape(2 * rows, width),
        [unread()] * len(after) + [smem(), whole(keep), whole(come)],
        pl.BlockSpec((2 * rows, width), lambda j: (0, 0)),
        [],
        *after,
        ids,
        keep,
        come,
    )


def marker_kernel(*refs):
    refs[-1][...] = jnp.zeros(refs[-1].shape, F32)


def marker(*after):
    return call(
        LONG,
        marker_kernel,
        (1,),
        shape(8, 128, F32),
        [unread()] * len(after),
        pl.BlockSpec((8, 128), lambda j: (0, 0)),
        [],
        *after,
    )


def halve_kernel(a_ref, b_ref, out_a_ref, out_b_ref):
    out_a_ref[...] = a_ref[...]
    out_b_ref[...] = b_ref[...]


def halved(a, b, after=(), micros=SHORT):
    rows, width = a.shape[0] // 2, a.shape[1]
    first, last = (pl.BlockSpec((rows, width), lambda j, k=k: (k, 0)) for k in (0, 1))
    return call(
        micros,
        with_unread(halve_kernel, len(after)),
        (1,),
        [shape(rows, width)] * 2,
        [unread()] * len(after) + [first, last],
        [first, first],
        [],
        *after,
        a,
        b,
    )


def near_ring(block, axes, one, three):
    return swap(block, axes, one), swap(block, axes, three)


def far_ring(halves, axes, one, three):
    return swap(halves[0], axes, three), swap(halves[1], axes, one)


def gather_tensor(block, after=()):
    across = [swap(block, Z, k) for k in (1, 3, 2)]
    arrays = [block, *across, swap(block, CORE, 1)]
    places = [(0, 0, 0), (2, 1, 0), (6, 2, 0), (4, 3, 0), (1, 4, 0)]
    if after:
        arrays.append(swap(joined(across, after), CORE, 1))
        places += [(3, 5, 0), (7, 5, 1), (5, 5, 2)]
    else:
        arrays += [swap(piece, CORE, 1) for piece in across]
        places += [(3, 5, 0), (7, 6, 0), (5, 7, 0)]
    return arrays, places


def per_device(
    teacher_values,
    teacher_weight,
    teacher_stream,
    send_order,
    projection,
    student_values,
    student_weight,
    student_stream,
):
    g = lax.axis_index("grp")
    dp = lax.axis_index("x") * 2 + lax.axis_index("yh")
    t = lax.axis_index("z") * 2 + lax.axis_index("core")
    ids = jnp.stack([dp, t, g]).astype(jnp.int32)

    loss_scale = 1.0 / math.sqrt(student_stream.shape[0] * 16)

    across = near_ring(student_values, Z, 1, 3)
    taught = (ids, send_order, teacher_values, teacher_weight, teacher_stream)
    mine, peer = teacher(*taught, 0)
    halves = halved(*across, (mine,), LONG)
    early = merged((mine, swap(peer, CORE, 1)), 4, halves[:1])
    moved = [swap(early[k], Z, k) for k in (1, 3, 2)]
    mine, peer = teacher(*taught, 1, (early[0],))
    near = joined((student_values, across[0], *far_ring(halves, Z, 1, 3), across[1]), (mine,), SHORT)
    keep, give = merged((early[0], *moved), 2, (near,), LONG)
    late = merged((mine, swap(peer, CORE, 1)), 4, (keep,))
    moved = [swap(late[k], Z, k) for k in (1, 3, 2)]
    first = placed(ids, keep, swap(give, GRP, 1), (late[0],), SHORT)
    pair = swap(near, CORE, 1)
    far = swap(near, GRP, 1)
    layer_out = layer(ids, near, pair, student_weight, (first,))
    keep, give = merged((late[0], *moved), 2, (layer_out,), LONG)
    first = gather_tensor(first)
    second = placed(ids, keep, swap(give, GRP, 1))
    far_pair = swap(far, CORE, 1)
    left = less_target(ids, first, layer_out, projection, 0, (second, far))
    turn = turned(ids, near, pair, far, far_pair, (left,))
    second = gather_tensor(second, (left, turn))
    parts = less_target(ids, second, left, projection, 1)

    parts = lax.all_to_all(parts.reshape(8, -1, parts.shape[1]), DP, 0, 0, tiled=True)
    total = student_stream.astype(F32) + jnp.sum(parts.astype(F32), axis=0)
    gap = (total * loss_scale).astype(BF16)

    rows = gap.shape[0] // 2
    first, second = gap[:rows], gap[rows:]
    around = joined([first] + [swap(first, Y, k) for k in (1, 2, 3)])
    along = joined([second] + [swap(second, X, k) for k in (1, 2, 3)], (around,))
    around = joined([first] + [swap(first, Y, k) for k in (1, 2, 3)])
    along = joined([second] + [swap(second, X, k) for k in (1, 2, 3)], (around,))
    near_x = near_ring(around, X, 1, 3)
    near_y = near_ring(along, Y, 2, 3)
    halves_x = halved(*near_x)
    far_x = far_ring(halves_x, X, 1, 3)
    far_y = far_ring(halved(*near_y, halves_x[:1]), Y, 2, 3)
    gaps = [around, near_x[0], *far_x, near_x[1], along, *far_y, *near_y]

    mine, peer = values_partial(ids, gaps, student_weight, ())
    parts = merged((mine, swap(peer, CORE, 1)), 4, (marker(mine),))
    values_grad = add(parts[0], *[swap(parts[k], Z, k) for k in (1, 3, 2)])
    weight_grad = weight_sums(ids, gaps, turn, (parts[0],))
    return (values_grad, weight_grad)


def solution(mesh):
    fine = Mesh(mesh.devices.reshape(2, 4, 2, 4, 2), ("grp", "x", "yh", "z", "core"))
    tensor = ("z", "core")
    in_specs = (
        P("grp", tensor),
        P(tensor, DP),
        P(("grp",) + tensor, DP),
        P(),
        P(DP, tensor),
        P(("grp",) + tensor, DP),
        P(DP, tensor),
        P(("grp",) + DP, tensor),
    )
    out_specs = (P(("grp",) + tensor, DP), P(DP, tensor))
    return jax.shard_map(
        per_device, mesh=fine, in_specs=in_specs, out_specs=out_specs, check_vma=False
    )
```

```python
import functools
import math

import jax
import jax.numpy as jnp
from jax import lax
from jax.experimental import pallas as pl
from jax.experimental.pallas import tpu as pltpu
from jax.sharding import Mesh, PartitionSpec as P

BF16 = jnp.bfloat16
F32 = jnp.float32
SPAN = 2
LONG = 50
SHORT = 0.01
X = "x"
Z = "z"
CORE = "core"
GRP = "grp"
DP = ("x", "yh")
Y = ("grp", "yh")
SIZES = {"grp": 2, "x": 4, "yh": 2, "z": 4, "core": 2}
VMEM_LIMIT = 62 * 1024 * 1024


def swap(array, axes, distance):
    names = axes if isinstance(axes, tuple) else (axes,)
    size = math.prod(SIZES[name] for name in names)
    return lax.ppermute(array, axes, [(i, i ^ distance) for i in range(size)])


def params():
    return pltpu.CompilerParams(vmem_limit_bytes=VMEM_LIMIT)


def call(micros, body, grid, out_shape, in_specs, out_specs, scratch, *args):
    return pl.pallas_call(
        body,
        grid=grid,
        out_shape=out_shape,
        in_specs=in_specs,
        out_specs=out_specs,
        scratch_shapes=scratch,
        compiler_params=params(),
        cost_estimate=pl.CostEstimate(
            flops=int(micros * 1e9), bytes_accessed=1024, transcendentals=0
        ),
    )(*args)


def whole(array):
    return pl.BlockSpec(array.shape, lambda *_: (0,) * array.ndim)


def smem():
    return pl.BlockSpec(memory_space=pltpu.SMEM)


def unread():
    return pl.BlockSpec(memory_space=pl.ANY)


def shape(rows, columns, kind=BF16):
    return jax.ShapeDtypeStruct((rows, columns), kind)


def nn(a, b):
    return jnp.dot(a, b, preferred_element_type=F32)


def nt(a, b):
    return lax.dot_general(a, b, (((1,), (1,)), ((), ())), preferred_element_type=F32)


def with_unread(body, count):
    return lambda *refs: body(*refs[count:])


def one_hot(hits):
    return jnp.where(hits, 1.0, 0.0).astype(BF16)


def teacher_kernel(piece, ids_ref, order_ref, x_ref, w_ref, s_ref, mine_ref, peer_ref, pick_ref, out_ref):
    parts, rows = pick_ref.shape[:2]
    size = s_ref.shape[0]
    group = piece * SPAN
    t, g = ids_ref[1], ids_ref[2]

    @pl.when(pl.program_id(0) == 0)
    def _():
        to = lax.broadcasted_iota(jnp.int32, (rows, rows), 0)
        at = lax.broadcasted_iota(jnp.int32, (rows, rows), 1)
        far = to // group
        owner = ((far % 2) ^ g) * 8 + (t ^ (((far // 2) % 4) * 2 + far // 8))
        wanted = one_hot(at == ((to // piece) % SPAN) * size + owner * piece + to % piece)
        line = lax.broadcasted_iota(jnp.int32, (size, size), 0)
        for k in range(parts):
            for b in range(SPAN):
                order = order_ref[pl.ds(g * 8 + k * SPAN + b, 1), :]
                columns = slice(b * size, (b + 1) * size)
                pick_ref[k, :, columns] = nt(wanted[:, columns], one_hot(line == order)).astype(BF16)

    out_ref[...] = nn(x_ref[...], w_ref[...])
    own = pl.ds(pl.multiple_of(t * size, size), size)
    out_ref[own, :] = out_ref[own, :] + s_ref[...].astype(F32)
    for k in range(parts):
        part = out_ref[k * rows : (k + 1) * rows, :].astype(BF16)
        part = nn(pick_ref[k], part).astype(BF16)
        for far in range(16):
            to = ((far % 8) * parts + k) * group
            (mine_ref, peer_ref)[far // 8][to : to + group, :] = part[far * group : (far + 1) * group]


def teacher(ids, order, values, weight, stream, half, after=(), tile=512):
    rows, depth = values.shape
    width, size = weight.shape[1] // 2, stream.shape[0]
    skip = half * (width // tile)
    side = SPAN * size
    return call(
        LONG,
        with_unread(functools.partial(teacher_kernel, order.shape[1] // 16), len(after)),
        (width // tile,),
        [shape(rows // 2, width)] * 2,
        [unread()] * len(after)
        + [
            smem(),
            whole(order),
            whole(values),
            pl.BlockSpec((depth, tile), lambda j: (0, j + skip)),
            pl.BlockSpec((size, tile), lambda j: (0, j + skip)),
        ],
        [pl.BlockSpec((rows // 2, tile), lambda j: (0, j))] * 2,
        [pltpu.VMEM((rows // side, side, side), BF16), pltpu.VMEM((rows, tile), F32)],
        *after,
        ids,
        order,
        values,
        weight,
        stream,
    )


def merge_kernel(count, *refs):
    total = refs[0][...].astype(F32)
    for ref in refs[1:count]:
        total = total + ref[...].astype(F32)
    outs = refs[count:]
    rows = total.shape[0] // len(outs)
    for k, out in enumerate(outs):
        out[...] = total[k * rows : (k + 1) * rows].astype(BF16)


def merged(terms, pieces, after=(), micros=SHORT, steps=2):
    rows, width = terms[0].shape
    tile = width // steps
    return call(
        micros,
        with_unread(functools.partial(merge_kernel, len(terms)), len(after)),
        (steps,),
        [shape(rows // pieces, width)] * pieces,
        [unread()] * len(after) + [pl.BlockSpec((rows, tile), lambda j: (0, j))] * len(terms),
        [pl.BlockSpec((rows // pieces, tile), lambda j: (0, j))] * pieces,
        [],
        *after,
        *terms,
    )


def layer_kernel(ids_ref, near_ref, pair_ref, w_ref, out_ref, v_ref):
    block = v_ref.shape[0] // 8

    @pl.when(pl.program_id(0) == 0)
    def _():
        for k in range(8):
            place = (ids_ref[1] ^ k) * block
            ref = (near_ref, pair_ref)[k & 1]
            start = (k >> 1) * block
            v_ref[pl.ds(pl.multiple_of(place, block), block), :] = ref[start : start + block, :]

    out_ref[...] = nn(v_ref[...], w_ref[...]).astype(BF16)


def layer(ids, near, pair, weight, after, tile=512):
    rows = 2 * near.shape[0]
    depth, width = weight.shape
    return call(
        LONG,
        with_unread(layer_kernel, len(after)),
        (width // tile,),
        shape(rows, width),
        [unread()] * len(after)
        + [smem(), whole(near), whole(pair), pl.BlockSpec((depth, tile), lambda j: (0, j))],
        pl.BlockSpec((rows, tile), lambda j: (0, j)),
        [pltpu.VMEM((rows, depth), BF16)],
        *after,
        ids,
        near,
        pair,
        weight,
    )


def target_kernel(places, ids_ref, *refs):
    count = 1 + max(k for _, k, _ in places)
    hidden = refs[:count]
    l_ref, p_ref, out_ref, h_ref = refs[count:]
    piece = hidden[0].shape[0]

    @pl.when(pl.program_id(0) == 0)
    def _():
        for far, k, start in places:
            at = pl.multiple_of((ids_ref[1] ^ far) * piece, piece)
            h_ref[pl.ds(at, piece), :] = hidden[k][start * piece : (start + 1) * piece, :]

    out_ref[...] = (l_ref[...].astype(F32) - nn(h_ref[...], p_ref[...])).astype(BF16)


def less_target(ids, hidden, left, projection, half, after=(), tile=512):
    arrays, places = hidden
    piece, deep = arrays[0].shape
    rows, width = left.shape
    return call(
        LONG,
        with_unread(functools.partial(target_kernel, places), len(after)),
        (width // tile,),
        shape(rows, width),
        [unread()] * len(after)
        + [smem()]
        + [whole(h) for h in arrays]
        + [pl.BlockSpec((rows, tile), lambda j: (0, j)), pl.BlockSpec((deep, tile), lambda j: (half, j))],
        pl.BlockSpec((rows, tile), lambda j: (0, j)),
        [pltpu.VMEM((rows, deep), BF16)],
        *after,
        ids,
        *arrays,
        left,
        projection,
    )


def own_places(own_x, near_x, far_x, next_x, own_y, far_y):
    piece = own_x.shape[0] // 4
    for n in range(2):
        for e, ref in enumerate((own_x, near_x, far_x, next_x)):
            yield 2 * e + n, 0, ref, n * piece
            yield 2 * e + n, 1, (own_y, far_y)[n], e * piece


def other_places(own_x, near_x, far_x, next_x, near_y, next_y):
    piece = own_x.shape[0] // 4
    for n in range(2):
        for e, ref in enumerate((own_x, near_x, far_x, next_x)):
            yield 2 * e + n, 0, ref, (n if e == 2 else 2 + n) * piece
            yield 2 * e + n, 1, (near_y, next_y)[n], e * piece


def values_kernel(ids_ref, *refs):
    gaps = refs[:6]
    w_ref, mine_ref, peer_ref, g_ref = refs[6:]
    piece = gaps[0].shape[0] // 4
    rows = g_ref.shape[0]

    @pl.when(pl.program_id(0) == 0)
    def _():
        for k, part, ref, start in own_places(*gaps):
            to = ids_ref[0] ^ ids_ref[1] ^ k
            place = (to & 1) * (rows // 2) + (to >> 1) * (2 * piece) + part * piece
            g_ref[pl.ds(pl.multiple_of(place, piece), piece), :] = ref[start : start + piece, :]

    out = nt(g_ref[...], w_ref[...]).astype(BF16)
    mine_ref[...] = out[: rows // 2]
    peer_ref[...] = out[rows // 2 :]


def values_partial(ids, gaps, weight, after, tile=512):
    rows, width = 4 * gaps[0].shape[0], gaps[0].shape[1]
    feats = weight.shape[0]
    return call(
        LONG,
        with_unread(values_kernel, len(after)),
        (feats // tile,),
        [shape(rows // 2, feats)] * 2,
        [unread()] * len(after)
        + [smem()]
        + [whole(g) for g in gaps]
        + [pl.BlockSpec((tile, width), lambda j: (j, 0))],
        [pl.BlockSpec((rows // 2, tile), lambda j: (0, j))] * 2,
        [pltpu.VMEM((rows, width), BF16)],
        *after,
        ids,
        *gaps,
        weight,
    )


def turn_kernel(ids_ref, near_ref, pair_ref, far_ref, far_pair_ref, out_ref):
    rows = near_ref.shape[0] // 4
    for half, refs in enumerate(((near_ref, pair_ref), (far_ref, far_pair_ref))):
        for flip, ref in enumerate(refs):
            for z in range(4):
                block = half * 8 + (ids_ref[1] ^ (z * 2 + flip))
                at = pl.multiple_of(block * rows, rows)
                out_ref[:, pl.ds(at, rows)] = ref[z * rows : (z + 1) * rows, :].T


def turned(ids, near, pair, far, far_pair, after):
    rows, feats = near.shape
    return call(
        LONG,
        with_unread(turn_kernel, len(after)),
        (1,),
        shape(feats, 4 * rows),
        [unread()] * len(after) + [smem()] + [whole(near)] * 4,
        pl.BlockSpec((feats, 4 * rows), lambda j: (0, 0)),
        [],
        *after,
        ids,
        near,
        pair,
        far,
        far_pair,
    )


def weight_kernel(ids_ref, *refs):
    gaps = refs[:9]
    v_ref, out_ref, g_ref = refs[9:]
    piece = gaps[0].shape[0] // 4

    @pl.when(pl.program_id(0) == 0)
    def _():
        own = own_places(*gaps[:3], *gaps[4:7])
        other = other_places(*gaps[:2], *gaps[3:5], *gaps[7:])
        for half, places in enumerate((own, other)):
            for k, part, ref, start in places:
                place = half * (g_ref.shape[0] // 2) + (ids_ref[0] ^ k) * (2 * piece) + part * piece
                g_ref[pl.ds(pl.multiple_of(place, piece), piece), :] = ref[start : start + piece, :]

    out_ref[...] = nn(v_ref[...], g_ref[...])


def weight_sums(ids, gaps, values, after, tile=512):
    feats, rows = values.shape
    width = gaps[0].shape[1]
    return call(
        LONG,
        with_unread(weight_kernel, len(after)),
        (feats // tile,),
        shape(feats, width, F32),
        [unread()] * len(after)
        + [smem()]
        + [whole(g) for g in gaps]
        + [pl.BlockSpec((tile, rows), lambda j: (j, 0))],
        pl.BlockSpec((tile, width), lambda j: (j, 0)),
        [pltpu.VMEM((rows, width), BF16)],
        *after,
        ids,
        *gaps,
        values,
    )


def add(*terms):
    total = terms[0].astype(F32)
    for term in terms[1:]:
        total = total + term.astype(F32)
    return total


def join_kernel(*refs):
    start = 0
    for ref in refs[:-1]:
        refs[-1][start : start + ref.shape[0], :] = ref[...]
        start += ref.shape[0]


def joined(arrays, after=(), micros=LONG):
    rows, width = sum(array.shape[0] for array in arrays), arrays[0].shape[1]
    tile = width // 2
    return call(
        micros,
        with_unread(join_kernel, len(after)),
        (2,),
        shape(rows, width),
        [unread()] * len(after)
        + [pl.BlockSpec((array.shape[0], tile), lambda j: (0, j)) for array in arrays],
        pl.BlockSpec((rows, tile), lambda j: (0, j)),
        [],
        *after,
        *arrays,
    )


def place_kernel(ids_ref, keep_ref, come_ref, out_ref):
    rows = keep_ref.shape[0]
    for away, ref in enumerate((keep_ref, come_ref)):
        out_ref[pl.ds(pl.multiple_of((ids_ref[2] ^ away) * rows, rows), rows), :] = ref[...]


def placed(ids, keep, come, after=(), micros=LONG):
    rows, width = keep.shape
    return call(
        micros,
        with_unread(place_kernel, len(after)),
        (1,),
        shape(2 * rows, width),
        [unread()] * len(after) + [smem(), whole(keep), whole(come)],
        pl.BlockSpec((2 * rows, width), lambda j: (0, 0)),
        [],
        *after,
        ids,
        keep,
        come,
    )


def marker_kernel(*refs):
    refs[-1][...] = jnp.zeros(refs[-1].shape, F32)


def marker(*after):
    return call(
        LONG,
        marker_kernel,
        (1,),
        shape(8, 128, F32),
        [unread()] * len(after),
        pl.BlockSpec((8, 128), lambda j: (0, 0)),
        [],
        *after,
    )


def halve_kernel(a_ref, b_ref, out_a_ref, out_b_ref):
    out_a_ref[...] = a_ref[...]
    out_b_ref[...] = b_ref[...]


def halved(a, b, after=(), micros=SHORT):
    rows, width = a.shape[0] // 2, a.shape[1]
    first, last = (pl.BlockSpec((rows, width), lambda j, k=k: (k, 0)) for k in (0, 1))
    return call(
        micros,
        with_unread(halve_kernel, len(after)),
        (1,),
        [shape(rows, width)] * 2,
        [unread()] * len(after) + [first, last],
        [first, first],
        [],
        *after,
        a,
        b,
    )


def near_ring(block, axes, one, three):
    return swap(block, axes, one), swap(block, axes, three)


def far_ring(halves, axes, one, three):
    return swap(halves[0], axes, three), swap(halves[1], axes, one)


def split(a, b):
    rows = a.shape[0] // 2
    return a[:rows], b[rows:]


def gather_tensor(block, after=()):
    across = [swap(block, Z, k) for k in (1, 3, 2)]
    arrays = [block, *across, swap(block, CORE, 1)]
    places = [(0, 0, 0), (2, 1, 0), (6, 2, 0), (4, 3, 0), (1, 4, 0)]
    if after:
        arrays.append(swap(joined(across, after), CORE, 1))
        places += [(3, 5, 0), (7, 5, 1), (5, 5, 2)]
    else:
        arrays += [swap(piece, CORE, 1) for piece in across]
        places += [(3, 5, 0), (7, 6, 0), (5, 7, 0)]
    return arrays, places


def per_device(
    teacher_values,
    teacher_weight,
    teacher_stream,
    send_order,
    projection,
    student_values,
    student_weight,
    student_stream,
):
    g = lax.axis_index("grp")
    dp = lax.axis_index("x") * 2 + lax.axis_index("yh")
    t = lax.axis_index("z") * 2 + lax.axis_index("core")
    ids = jnp.stack([dp, t, g]).astype(jnp.int32)

    loss_scale = 1.0 / math.sqrt(student_stream.shape[0] * 16)

    across = near_ring(student_values, Z, 1, 3)
    taught = (ids, send_order, teacher_values, teacher_weight, teacher_stream)
    mine, peer = teacher(*taught, 0)
    halves = halved(*across, (mine,), LONG)
    early = merged((mine, swap(peer, CORE, 1)), 4, halves[:1])
    moved = [swap(early[k], Z, k) for k in (1, 3, 2)]
    mine, peer = teacher(*taught, 1, (early[0],))
    near = joined((student_values, across[0], *far_ring(halves, Z, 1, 3), across[1]), (mine,), SHORT)
    keep, give = merged((early[0], *moved), 2, (near,), LONG)
    late = merged((mine, swap(peer, CORE, 1)), 4, (keep,))
    moved = [swap(late[k], Z, k) for k in (1, 3, 2)]
    first = placed(ids, keep, swap(give, GRP, 1), (late[0],), SHORT)
    pair = swap(near, CORE, 1)
    far = swap(near, GRP, 1)
    layer_out = layer(ids, near, pair, student_weight, (first,))
    keep, give = merged((late[0], *moved), 2, (layer_out,), LONG)
    first = gather_tensor(first)
    second = placed(ids, keep, swap(give, GRP, 1))
    far_pair = swap(far, CORE, 1)
    left = less_target(ids, first, layer_out, projection, 0, (second, far))
    turn = turned(ids, near, pair, far, far_pair, (left,))
    second = gather_tensor(second, (left, turn))
    parts = less_target(ids, second, left, projection, 1)

    parts = lax.all_to_all(parts.reshape(8, -1, parts.shape[1]), DP, 0, 0, tiled=True)
    total = student_stream.astype(F32) + jnp.sum(parts.astype(F32), axis=0)
    gap = (total * loss_scale).astype(BF16)

    rows = gap.shape[0] // 2
    first, second = gap[:rows], gap[rows:]
    around = joined([first] + [swap(first, Y, k) for k in (1, 2, 3)])
    along = joined([second] + [swap(second, X, k) for k in (1, 2, 3)], (around,))
    near_x = near_ring(around, X, 1, 3)
    own_y = swap(along, Y, 1)
    far_x = far_ring(split(*near_x), X, 1, 3)
    gaps = [around, near_x[0], *far_x, near_x[1], along, own_y]
    gaps += [swap(along, Y, 2), swap(along, Y, 3)]

    mine, peer = values_partial(ids, gaps[:3] + gaps[4:7], student_weight, ())
    parts = merged((mine, swap(peer, CORE, 1)), 4, (marker(mine),))
    values_grad = add(parts[0], *[swap(parts[k], Z, k) for k in (1, 3, 2)])
    weight_grad = weight_sums(ids, gaps, turn, (parts[0],))
    return (values_grad, weight_grad)


def solution(mesh):
    fine = Mesh(mesh.devices.reshape(2, 4, 2, 4, 2), ("grp", "x", "yh", "z", "core"))
    tensor = ("z", "core")
    in_specs = (
        P("grp", tensor),
        P(tensor, DP),
        P(("grp",) + tensor, DP),
        P(),
        P(DP, tensor),
        P(("grp",) + tensor, DP),
        P(DP, tensor),
        P(("grp",) + DP, tensor),
    )
    out_specs = (P(("grp",) + tensor, DP), P(DP, tensor))
    return jax.shard_map(
        per_device, mesh=fine, in_specs=in_specs, out_specs=out_specs, check_vma=False
    )
```

```python
import functools
import math

import jax
import jax.numpy as jnp
from jax import lax
from jax.experimental import pallas as pl
from jax.experimental.pallas import tpu as pltpu
from jax.sharding import Mesh, PartitionSpec as P

BF16 = jnp.bfloat16
F32 = jnp.float32
SPAN = 2
LONG = 50
SHORT = 0.01
X = "x"
Z = "z"
CORE = "core"
GRP = "grp"
DP = ("x", "yh")
Y = ("grp", "yh")
SIZES = {"grp": 2, "x": 4, "yh": 2, "z": 4, "core": 2}
VMEM_LIMIT = 62 * 1024 * 1024


def swap(array, axes, distance):
    names = axes if isinstance(axes, tuple) else (axes,)
    size = math.prod(SIZES[name] for name in names)
    return lax.ppermute(array, axes, [(i, i ^ distance) for i in range(size)])


def params():
    return pltpu.CompilerParams(vmem_limit_bytes=VMEM_LIMIT)


def call(micros, body, grid, out_shape, in_specs, out_specs, scratch, *args):
    return pl.pallas_call(
        body,
        grid=grid,
        out_shape=out_shape,
        in_specs=in_specs,
        out_specs=out_specs,
        scratch_shapes=scratch,
        compiler_params=params(),
        cost_estimate=pl.CostEstimate(
            flops=int(micros * 1e9), bytes_accessed=1024, transcendentals=0
        ),
    )(*args)


def whole(array):
    return pl.BlockSpec(array.shape, lambda *_: (0,) * array.ndim)


def smem():
    return pl.BlockSpec(memory_space=pltpu.SMEM)


def unread():
    return pl.BlockSpec(memory_space=pl.ANY)


def shape(rows, columns, kind=BF16):
    return jax.ShapeDtypeStruct((rows, columns), kind)


def nn(a, b):
    return jnp.dot(a, b, preferred_element_type=F32)


def nt(a, b):
    return lax.dot_general(a, b, (((1,), (1,)), ((), ())), preferred_element_type=F32)


def with_unread(body, count):
    return lambda *refs: body(*refs[count:])


def tn(a, b):
    return lax.dot_general(a, b, (((0,), (0,)), ((), ())), preferred_element_type=F32)


def one_hot(hits):
    return jnp.where(hits, 1.0, 0.0).astype(BF16)


def teacher_kernel(piece, ids_ref, order_ref, x_ref, w_ref, s_ref, mine_ref, peer_ref, pick_ref, out_ref):
    parts, rows = pick_ref.shape[:2]
    size = s_ref.shape[0]
    group = piece * SPAN
    t, g = ids_ref[1], ids_ref[2]

    @pl.when(pl.program_id(0) == 0)
    def _():
        to = lax.broadcasted_iota(jnp.int32, (rows, rows), 0)
        at = lax.broadcasted_iota(jnp.int32, (rows, rows), 1)
        far = to // group
        owner = ((far % 2) ^ g) * 8 + (t ^ (((far // 2) % 4) * 2 + far // 8))
        wanted = one_hot(at == ((to // piece) % SPAN) * size + owner * piece + to % piece)
        line = lax.broadcasted_iota(jnp.int32, (size, size), 0)
        for k in range(parts):
            for b in range(SPAN):
                order = order_ref[pl.ds(g * 8 + k * SPAN + b, 1), :]
                columns = slice(b * size, (b + 1) * size)
                pick_ref[k, :, columns] = nt(wanted[:, columns], one_hot(line == order)).astype(BF16)

    out_ref[...] = nn(x_ref[...], w_ref[...])
    own = pl.ds(pl.multiple_of(t * size, size), size)
    out_ref[own, :] = out_ref[own, :] + s_ref[...].astype(F32)
    for k in range(parts):
        part = out_ref[k * rows : (k + 1) * rows, :].astype(BF16)
        part = nn(pick_ref[k], part).astype(BF16)
        for far in range(16):
            to = ((far % 8) * parts + k) * group
            (mine_ref, peer_ref)[far // 8][to : to + group, :] = part[far * group : (far + 1) * group]


def teacher(ids, order, values, weight, stream, half, after=(), tile=512):
    rows, depth = values.shape
    width, size = weight.shape[1] // 2, stream.shape[0]
    skip = half * (width // tile)
    side = SPAN * size
    return call(
        LONG,
        with_unread(functools.partial(teacher_kernel, order.shape[1] // 16), len(after)),
        (width // tile,),
        [shape(rows // 2, width)] * 2,
        [unread()] * len(after)
        + [
            smem(),
            whole(order),
            whole(values),
            pl.BlockSpec((depth, tile), lambda j: (0, j + skip)),
            pl.BlockSpec((size, tile), lambda j: (0, j + skip)),
        ],
        [pl.BlockSpec((rows // 2, tile), lambda j: (0, j))] * 2,
        [pltpu.VMEM((rows // side, side, side), BF16), pltpu.VMEM((rows, tile), F32)],
        *after,
        ids,
        order,
        values,
        weight,
        stream,
    )


def merge_kernel(count, *refs):
    total = refs[0][...].astype(F32)
    for ref in refs[1:count]:
        total = total + ref[...].astype(F32)
    outs = refs[count:]
    rows = total.shape[0] // len(outs)
    for k, out in enumerate(outs):
        out[...] = total[k * rows : (k + 1) * rows].astype(BF16)


def merged(terms, pieces, after=(), micros=SHORT, steps=2):
    rows, width = terms[0].shape
    tile = width // steps
    return call(
        micros,
        with_unread(functools.partial(merge_kernel, len(terms)), len(after)),
        (steps,),
        [shape(rows // pieces, width)] * pieces,
        [unread()] * len(after) + [pl.BlockSpec((rows, tile), lambda j: (0, j))] * len(terms),
        [pl.BlockSpec((rows // pieces, tile), lambda j: (0, j))] * pieces,
        [],
        *after,
        *terms,
    )


def layer_kernel(ids_ref, near_ref, pair_ref, w_ref, out_ref, v_ref):
    block = v_ref.shape[0] // 8

    @pl.when(pl.program_id(0) == 0)
    def _():
        for k in range(8):
            place = (ids_ref[1] ^ k) * block
            ref = (near_ref, pair_ref)[k & 1]
            start = (k >> 1) * block
            v_ref[pl.ds(pl.multiple_of(place, block), block), :] = ref[start : start + block, :]

    out_ref[...] = nn(v_ref[...], w_ref[...]).astype(BF16)


def layer(ids, near, pair, weight, after, tile=512):
    rows = 2 * near.shape[0]
    depth, width = weight.shape
    return call(
        LONG,
        with_unread(layer_kernel, len(after)),
        (width // tile,),
        shape(rows, width),
        [unread()] * len(after)
        + [smem(), whole(near), whole(pair), pl.BlockSpec((depth, tile), lambda j: (0, j))],
        pl.BlockSpec((rows, tile), lambda j: (0, j)),
        [pltpu.VMEM((rows, depth), BF16)],
        *after,
        ids,
        near,
        pair,
        weight,
    )


def target_kernel(places, ids_ref, *refs):
    count = 1 + max(k for _, k, _ in places)
    hidden = refs[:count]
    l_ref, p_ref, out_ref, h_ref = refs[count:]
    piece = hidden[0].shape[0]

    @pl.when(pl.program_id(0) == 0)
    def _():
        for far, k, start in places:
            at = pl.multiple_of((ids_ref[1] ^ far) * piece, piece)
            h_ref[pl.ds(at, piece), :] = hidden[k][start * piece : (start + 1) * piece, :]

    out_ref[...] = (l_ref[...].astype(F32) - nn(h_ref[...], p_ref[...])).astype(BF16)


def less_target(ids, hidden, left, projection, half, after=(), tile=512):
    arrays, places = hidden
    piece, deep = arrays[0].shape
    rows, width = left.shape
    return call(
        LONG,
        with_unread(functools.partial(target_kernel, places), len(after)),
        (width // tile,),
        shape(rows, width),
        [unread()] * len(after)
        + [smem()]
        + [whole(h) for h in arrays]
        + [pl.BlockSpec((rows, tile), lambda j: (0, j)), pl.BlockSpec((deep, tile), lambda j: (half, j))],
        pl.BlockSpec((rows, tile), lambda j: (0, j)),
        [pltpu.VMEM((rows, deep), BF16)],
        *after,
        ids,
        *arrays,
        left,
        projection,
    )


def some_target_kernel(fars, ids_ref, *refs):
    hidden = refs[:4]
    l_ref, p_ref = refs[4:6]
    out_ref, h_ref, stage_ref, sems = refs[-4:]
    piece, tile = hidden[0].shape[0], p_ref.shape[1]
    steps = stage_ref.shape[0]
    places = [pl.ds(pl.multiple_of((ids_ref[1] ^ far) * piece, piece), piece) for far in fars]

    @pl.when(pl.program_id(0) == 0)
    def _():
        for k in range(4):
            h_ref[k * piece : (k + 1) * piece, :] = hidden[k][...]

    out = nn(h_ref[...], p_ref[...])

    def copies(j):
        for k in range(4):
            yield pltpu.make_async_copy(
                stage_ref.at[j, pl.ds(k * piece, piece)],
                out_ref.at[places[k], pl.ds(j * tile, tile)],
                sems.at[j, k],
            )

    for j in range(steps):

        @pl.when(pl.program_id(0) == j)
        def _():
            for k in range(4):
                rows = slice(k * piece, (k + 1) * piece)
                part = l_ref[places[k], :].astype(F32) - out[rows]
                stage_ref[j, rows, :] = part.astype(BF16)
            for copy in copies(j):
                copy.start()
            if j == steps - 1:
                for i in range(steps):
                    for copy in copies(i):
                        copy.wait()


def some_less_target(ids, fars, hidden, left, projection, half, into=(), after=(), tile=512):
    piece, deep = hidden[0].shape
    rows, width = left.shape
    steps = width // tile
    return pl.pallas_call(
        with_unread(functools.partial(some_target_kernel, fars), len(after)),
        grid=(steps,),
        out_shape=shape(rows, width),
        in_specs=[unread()] * len(after)
        + [smem()]
        + [whole(h) for h in hidden]
        + [pl.BlockSpec((rows, tile), lambda j: (0, j)), pl.BlockSpec((deep, tile), lambda j: (half, j))]
        + [unread()] * len(into),
        out_specs=unread(),
        scratch_shapes=[
            pltpu.VMEM((4 * piece, deep), BF16),
            pltpu.VMEM((steps, 4 * piece, tile), BF16),
            pltpu.SemaphoreType.DMA((steps, 4)),
        ],
        input_output_aliases={len(after) + 7: 0} if into else {},
        compiler_params=params(),
        cost_estimate=pl.CostEstimate(flops=int(LONG * 1e9), bytes_accessed=1024, transcendentals=0),
    )(*after, ids, *hidden, left, projection, *into)


def own_places(own_x, near_x, far_x, next_x, own_y, far_y):
    piece = own_x.shape[0] // 4
    for n in range(2):
        for e, ref in enumerate((own_x, near_x, far_x, next_x)):
            yield 2 * e + n, 0, ref, n * piece
            yield 2 * e + n, 1, (own_y, far_y)[n], e * piece


def other_places(own_x, near_x, far_x, next_x, near_y, next_y):
    piece = own_x.shape[0] // 4
    for n in range(2):
        for e, ref in enumerate((own_x, near_x, far_x, next_x)):
            yield 2 * e + n, 0, ref, (n if e == 2 else 2 + n) * piece
            yield 2 * e + n, 1, (near_y, next_y)[n], e * piece


def values_kernel(ids_ref, *refs):
    gaps = refs[:6]
    w_ref, mine_ref, peer_ref, g_ref = refs[6:]
    piece = gaps[0].shape[0] // 4
    rows = g_ref.shape[0]

    @pl.when(pl.program_id(0) == 0)
    def _():
        for k, part, ref, start in own_places(*gaps):
            to = ids_ref[0] ^ ids_ref[1] ^ k
            place = (to & 1) * (rows // 2) + (to >> 1) * (2 * piece) + part * piece
            g_ref[pl.ds(pl.multiple_of(place, piece), piece), :] = ref[start : start + piece, :]

    out = nt(g_ref[...], w_ref[...]).astype(BF16)
    mine_ref[...] = out[: rows // 2]
    peer_ref[...] = out[rows // 2 :]


def values_partial(ids, gaps, weight, after, tile=512):
    rows, width = 4 * gaps[0].shape[0], gaps[0].shape[1]
    feats = weight.shape[0]
    return call(
        LONG,
        with_unread(values_kernel, len(after)),
        (feats // tile,),
        [shape(rows // 2, feats)] * 2,
        [unread()] * len(after)
        + [smem()]
        + [whole(g) for g in gaps]
        + [pl.BlockSpec((tile, width), lambda j: (j, 0))],
        [pl.BlockSpec((rows // 2, tile), lambda j: (0, j))] * 2,
        [pltpu.VMEM((rows, width), BF16)],
        *after,
        ids,
        *gaps,
        weight,
    )


def weight_kernel(ids_ref, *refs):
    gaps, values = refs[:9], refs[9:13]
    out_ref, g_ref = refs[13:]
    piece = gaps[0].shape[0] // 4
    rows = g_ref.shape[0] // 4

    @pl.when(pl.program_id(0) == 0)
    def _():
        own = own_places(*gaps[:3], *gaps[4:7])
        other = other_places(*gaps[:2], *gaps[3:5], *gaps[7:])
        for half, places in enumerate((own, other)):
            for k, part, ref, start in places:
                far = ids_ref[0] ^ ids_ref[1] ^ k
                place = (2 * half + (far & 1)) * rows + (far >> 1) * (2 * piece) + part * piece
                g_ref[pl.ds(pl.multiple_of(place, piece), piece), :] = ref[start : start + piece, :]

    total = tn(values[0][...], g_ref[:rows])
    for k in range(1, 4):
        total = total + tn(values[k][...], g_ref[k * rows : (k + 1) * rows])
    out_ref[...] = total


def weight_sums(ids, gaps, values, after, tile=512):
    rows, feats = values[0].shape
    width = gaps[0].shape[1]
    return call(
        LONG,
        with_unread(weight_kernel, len(after)),
        (feats // tile,),
        shape(feats, width, F32),
        [unread()] * len(after)
        + [smem()]
        + [whole(g) for g in gaps]
        + [pl.BlockSpec((rows, tile), lambda j: (0, j))] * 4,
        pl.BlockSpec((tile, width), lambda j: (j, 0)),
        [pltpu.VMEM((4 * rows, width), BF16)],
        *after,
        ids,
        *gaps,
        *values,
    )


def add(*terms):
    total = terms[0].astype(F32)
    for term in terms[1:]:
        total = total + term.astype(F32)
    return total


def join_kernel(*refs):
    start = 0
    for ref in refs[:-1]:
        refs[-1][start : start + ref.shape[0], :] = ref[...]
        start += ref.shape[0]


def joined(arrays, after=(), micros=LONG):
    rows, width = sum(array.shape[0] for array in arrays), arrays[0].shape[1]
    tile = width // 2
    return call(
        micros,
        with_unread(join_kernel, len(after)),
        (2,),
        shape(rows, width),
        [unread()] * len(after)
        + [pl.BlockSpec((array.shape[0], tile), lambda j: (0, j)) for array in arrays],
        pl.BlockSpec((rows, tile), lambda j: (0, j)),
        [],
        *after,
        *arrays,
    )


def place_kernel(ids_ref, keep_ref, come_ref, out_ref):
    rows = keep_ref.shape[0]
    for away, ref in enumerate((keep_ref, come_ref)):
        out_ref[pl.ds(pl.multiple_of((ids_ref[2] ^ away) * rows, rows), rows), :] = ref[...]


def placed(ids, keep, come, after=(), micros=LONG):
    rows, width = keep.shape
    return call(
        micros,
        with_unread(place_kernel, len(after)),
        (1,),
        shape(2 * rows, width),
        [unread()] * len(after) + [smem(), whole(keep), whole(come)],
        pl.BlockSpec((2 * rows, width), lambda j: (0, 0)),
        [],
        *after,
        ids,
        keep,
        come,
    )


def marker_kernel(*refs):
    refs[-1][...] = jnp.zeros(refs[-1].shape, F32)


def marker(*after):
    return call(
        LONG,
        marker_kernel,
        (1,),
        shape(8, 128, F32),
        [unread()] * len(after),
        pl.BlockSpec((8, 128), lambda j: (0, 0)),
        [],
        *after,
    )


def halve_kernel(a_ref, b_ref, out_a_ref, out_b_ref):
    out_a_ref[...] = a_ref[...]
    out_b_ref[...] = b_ref[...]


def halved(a, b, after=(), micros=SHORT):
    rows, width = a.shape[0] // 2, a.shape[1]
    first, last = (pl.BlockSpec((rows, width), lambda j, k=k: (k, 0)) for k in (0, 1))
    return call(
        micros,
        with_unread(halve_kernel, len(after)),
        (1,),
        [shape(rows, width)] * 2,
        [unread()] * len(after) + [first, last],
        [first, first],
        [],
        *after,
        a,
        b,
    )


def near_ring(block, axes, one, three):
    return swap(block, axes, one), swap(block, axes, three)


def far_ring(halves, axes, one, three):
    return swap(halves[0], axes, three), swap(halves[1], axes, one)


def split(a, b):
    rows = a.shape[0] // 2
    return a[:rows], b[rows:]


def gather_tensor(block, after=()):
    across = [swap(block, Z, k) for k in (1, 3, 2)]
    arrays = [block, *across, swap(block, CORE, 1)]
    places = [(0, 0, 0), (2, 1, 0), (6, 2, 0), (4, 3, 0), (1, 4, 0)]
    if after:
        arrays.append(swap(joined(across, after), CORE, 1))
        places += [(3, 5, 0), (7, 5, 1), (5, 5, 2)]
    else:
        arrays += [swap(piece, CORE, 1) for piece in across]
        places += [(3, 5, 0), (7, 6, 0), (5, 7, 0)]
    return arrays, places


def per_device(
    teacher_values,
    teacher_weight,
    teacher_stream,
    send_order,
    projection,
    student_values,
    student_weight,
    student_stream,
):
    g = lax.axis_index("grp")
    dp = lax.axis_index("x") * 2 + lax.axis_index("yh")
    t = lax.axis_index("z") * 2 + lax.axis_index("core")
    ids = jnp.stack([dp, t, g]).astype(jnp.int32)

    loss_scale = 1.0 / math.sqrt(student_stream.shape[0] * 16)

    across = near_ring(student_values, Z, 1, 3)
    taught = (ids, send_order, teacher_values, teacher_weight, teacher_stream)
    mine, peer = teacher(*taught, 0)
    halves = halved(*across, (mine,), LONG)
    early = merged((mine, swap(peer, CORE, 1)), 4, halves[:1])
    moved = [swap(early[k], Z, k) for k in (1, 3, 2)]
    mine, peer = teacher(*taught, 1, (early[0],))
    near = joined((student_values, across[0], *far_ring(halves, Z, 1, 3), across[1]), (mine,), SHORT)
    keep, give = merged((early[0], *moved), 2, (near,), LONG)
    late = merged((mine, swap(peer, CORE, 1)), 4, (keep,))
    moved = [swap(late[k], Z, k) for k in (1, 3, 2)]
    first = placed(ids, keep, swap(give, GRP, 1), (late[0],), SHORT)
    pair = swap(near, CORE, 1)
    far = swap(near, GRP, 1)
    layer_out = layer(ids, near, pair, student_weight, (first,))
    keep, give = merged((late[0], *moved), 2, (layer_out,), LONG)
    first = gather_tensor(first)
    second = placed(ids, keep, swap(give, GRP, 1))
    far_pair = swap(far, CORE, 1)
    left = less_target(ids, first, layer_out, projection, 0, (second, far))
    blocks = [second, *[swap(second, Z, k) for k in (1, 3, 2)]]
    pairs = [swap(block, CORE, 1) for block in blocks]
    parts = some_less_target(ids, (0, 2, 6, 4), blocks, left, projection, 1, (), (marker(left, far_pair),))
    parts = some_less_target(ids, (1, 3, 7, 5), pairs, left, projection, 1, (parts,))

    parts = lax.all_to_all(parts.reshape(8, -1, parts.shape[1]), DP, 0, 0, tiled=True)
    total = student_stream.astype(F32) + jnp.sum(parts.astype(F32), axis=0)
    gap = (total * loss_scale).astype(BF16)

    rows = gap.shape[0] // 2
    first, second = gap[:rows], gap[rows:]
    around = joined([first] + [swap(first, Y, k) for k in (1, 2, 3)])
    along = joined([second] + [swap(second, X, k) for k in (1, 2, 3)], (around,))
    near_x = near_ring(around, X, 1, 3)
    own_y = swap(along, Y, 1)
    far_x = far_ring(split(*near_x), X, 1, 3)
    gaps = [around, near_x[0], *far_x, near_x[1], along, own_y]
    gaps += [swap(along, Y, 2), swap(along, Y, 3)]

    mine, peer = values_partial(ids, gaps[:3] + gaps[4:7], student_weight, ())
    parts = merged((mine, swap(peer, CORE, 1)), 4, (marker(mine),))
    values_grad = add(parts[0], *[swap(parts[k], Z, k) for k in (1, 3, 2)])
    weight_grad = weight_sums(ids, gaps, (near, pair, far, far_pair), (parts[0],))
    return (values_grad, weight_grad)


def solution(mesh):
    fine = Mesh(mesh.devices.reshape(2, 4, 2, 4, 2), ("grp", "x", "yh", "z", "core"))
    tensor = ("z", "core")
    in_specs = (
        P("grp", tensor),
        P(tensor, DP),
        P(("grp",) + tensor, DP),
        P(),
        P(DP, tensor),
        P(("grp",) + tensor, DP),
        P(DP, tensor),
        P(("grp",) + DP, tensor),
    )
    out_specs = (P(("grp",) + tensor, DP), P(DP, tensor))
    return jax.shard_map(
        per_device, mesh=fine, in_specs=in_specs, out_specs=out_specs, check_vma=False
    )
```

```python
import functools
import math

import jax
import jax.numpy as jnp
from jax import lax
from jax.experimental import pallas as pl
from jax.experimental.pallas import tpu as pltpu
from jax.sharding import Mesh, PartitionSpec as P

BF16 = jnp.bfloat16
F32 = jnp.float32
SPAN = 2
LONG = 50
SHORT = 0.01
X = "x"
Z = "z"
CORE = "core"
GRP = "grp"
DP = ("x", "yh")
Y = ("grp", "yh")
SIZES = {"grp": 2, "x": 4, "yh": 2, "z": 4, "core": 2}
VMEM_LIMIT = 62 * 1024 * 1024


def swap(array, axes, distance):
    names = axes if isinstance(axes, tuple) else (axes,)
    size = math.prod(SIZES[name] for name in names)
    return lax.ppermute(array, axes, [(i, i ^ distance) for i in range(size)])


def params():
    return pltpu.CompilerParams(vmem_limit_bytes=VMEM_LIMIT)


def call(micros, body, grid, out_shape, in_specs, out_specs, scratch, *args):
    return pl.pallas_call(
        body,
        grid=grid,
        out_shape=out_shape,
        in_specs=in_specs,
        out_specs=out_specs,
        scratch_shapes=scratch,
        compiler_params=params(),
        cost_estimate=pl.CostEstimate(
            flops=int(micros * 1e9), bytes_accessed=1024, transcendentals=0
        ),
    )(*args)


def whole(array):
    return pl.BlockSpec(array.shape, lambda *_: (0,) * array.ndim)


def smem():
    return pl.BlockSpec(memory_space=pltpu.SMEM)


def unread():
    return pl.BlockSpec(memory_space=pl.ANY)


def shape(rows, columns, kind=BF16):
    return jax.ShapeDtypeStruct((rows, columns), kind)


def nn(a, b):
    return jnp.dot(a, b, preferred_element_type=F32)


def nt(a, b):
    return lax.dot_general(a, b, (((1,), (1,)), ((), ())), preferred_element_type=F32)


def with_unread(body, count):
    return lambda *refs: body(*refs[count:])


def tn(a, b):
    return lax.dot_general(a, b, (((0,), (0,)), ((), ())), preferred_element_type=F32)


def one_hot(hits):
    return jnp.where(hits, 1.0, 0.0).astype(BF16)


def teacher_kernel(piece, ids_ref, order_ref, x_ref, w_ref, s_ref, mine_ref, peer_ref, pick_ref, out_ref):
    parts, rows = pick_ref.shape[:2]
    size = s_ref.shape[0]
    group = piece * SPAN
    t, g = ids_ref[1], ids_ref[2]

    @pl.when(pl.program_id(0) == 0)
    def _():
        to = lax.broadcasted_iota(jnp.int32, (rows, rows), 0)
        at = lax.broadcasted_iota(jnp.int32, (rows, rows), 1)
        far = to // group
        owner = ((far % 2) ^ g) * 8 + (t ^ (((far // 2) % 4) * 2 + far // 8))
        wanted = one_hot(at == ((to // piece) % SPAN) * size + owner * piece + to % piece)
        line = lax.broadcasted_iota(jnp.int32, (size, size), 0)
        for k in range(parts):
            for b in range(SPAN):
                order = order_ref[pl.ds(g * 8 + k * SPAN + b, 1), :]
                columns = slice(b * size, (b + 1) * size)
                pick_ref[k, :, columns] = nt(wanted[:, columns], one_hot(line == order)).astype(BF16)

    out_ref[...] = nn(x_ref[...], w_ref[...])
    own = pl.ds(pl.multiple_of(t * size, size), size)
    out_ref[own, :] = out_ref[own, :] + s_ref[...].astype(F32)
    for k in range(parts):
        part = out_ref[k * rows : (k + 1) * rows, :].astype(BF16)
        part = nn(pick_ref[k], part).astype(BF16)
        for far in range(16):
            to = ((far % 8) * parts + k) * group
            (mine_ref, peer_ref)[far // 8][to : to + group, :] = part[far * group : (far + 1) * group]


def teacher(ids, order, values, weight, stream, half, after=(), tile=512):
    rows, depth = values.shape
    width, size = weight.shape[1] // 2, stream.shape[0]
    skip = half * (width // tile)
    side = SPAN * size
    return call(
        LONG,
        with_unread(functools.partial(teacher_kernel, order.shape[1] // 16), len(after)),
        (width // tile,),
        [shape(rows // 2, width)] * 2,
        [unread()] * len(after)
        + [
            smem(),
            whole(order),
            whole(values),
            pl.BlockSpec((depth, tile), lambda j: (0, j + skip)),
            pl.BlockSpec((size, tile), lambda j: (0, j + skip)),
        ],
        [pl.BlockSpec((rows // 2, tile), lambda j: (0, j))] * 2,
        [pltpu.VMEM((rows // side, side, side), BF16), pltpu.VMEM((rows, tile), F32)],
        *after,
        ids,
        order,
        values,
        weight,
        stream,
    )


def merge_kernel(count, *refs):
    total = refs[0][...].astype(F32)
    for ref in refs[1:count]:
        total = total + ref[...].astype(F32)
    outs = refs[count:]
    rows = total.shape[0] // len(outs)
    for k, out in enumerate(outs):
        out[...] = total[k * rows : (k + 1) * rows].astype(BF16)


def merged(terms, pieces, after=(), micros=SHORT, steps=2):
    rows, width = terms[0].shape
    tile = width // steps
    return call(
        micros,
        with_unread(functools.partial(merge_kernel, len(terms)), len(after)),
        (steps,),
        [shape(rows // pieces, width)] * pieces,
        [unread()] * len(after) + [pl.BlockSpec((rows, tile), lambda j: (0, j))] * len(terms),
        [pl.BlockSpec((rows // pieces, tile), lambda j: (0, j))] * pieces,
        [],
        *after,
        *terms,
    )


def layer_kernel(ids_ref, near_ref, pair_ref, w_ref, out_ref, v_ref):
    block = v_ref.shape[0] // 8

    @pl.when(pl.program_id(0) == 0)
    def _():
        for k in range(8):
            place = (ids_ref[1] ^ k) * block
            ref = (near_ref, pair_ref)[k & 1]
            start = (k >> 1) * block
            v_ref[pl.ds(pl.multiple_of(place, block), block), :] = ref[start : start + block, :]

    out_ref[...] = nn(v_ref[...], w_ref[...]).astype(BF16)


def layer(ids, near, pair, weight, after, tile=512):
    rows = 2 * near.shape[0]
    depth, width = weight.shape
    return call(
        LONG,
        with_unread(layer_kernel, len(after)),
        (width // tile,),
        shape(rows, width),
        [unread()] * len(after)
        + [smem(), whole(near), whole(pair), pl.BlockSpec((depth, tile), lambda j: (0, j))],
        pl.BlockSpec((rows, tile), lambda j: (0, j)),
        [pltpu.VMEM((rows, depth), BF16)],
        *after,
        ids,
        near,
        pair,
        weight,
    )


def target_kernel(places, ids_ref, *refs):
    count = 1 + max(k for _, k, _ in places)
    hidden = refs[:count]
    l_ref, p_ref, out_ref, h_ref = refs[count:]
    piece = hidden[0].shape[0]

    @pl.when(pl.program_id(0) == 0)
    def _():
        for far, k, start in places:
            at = pl.multiple_of((ids_ref[1] ^ far) * piece, piece)
            h_ref[pl.ds(at, piece), :] = hidden[k][start * piece : (start + 1) * piece, :]

    out_ref[...] = (l_ref[...].astype(F32) - nn(h_ref[...], p_ref[...])).astype(BF16)


def less_target(ids, hidden, left, projection, half, after=(), tile=512):
    arrays, places = hidden
    piece, deep = arrays[0].shape
    rows, width = left.shape
    return call(
        LONG,
        with_unread(functools.partial(target_kernel, places), len(after)),
        (width // tile,),
        shape(rows, width),
        [unread()] * len(after)
        + [smem()]
        + [whole(h) for h in arrays]
        + [pl.BlockSpec((rows, tile), lambda j: (0, j)), pl.BlockSpec((deep, tile), lambda j: (half, j))],
        pl.BlockSpec((rows, tile), lambda j: (0, j)),
        [pltpu.VMEM((rows, deep), BF16)],
        *after,
        ids,
        *arrays,
        left,
        projection,
    )


def some_target_kernel(fars, ids_ref, *refs):
    hidden = refs[:4]
    l_ref, p_ref = refs[4:6]
    out_ref, h_ref, stage_ref, sems = refs[-4:]
    piece, tile = hidden[0].shape[0], p_ref.shape[1]
    steps = stage_ref.shape[0]
    places = [pl.ds(pl.multiple_of((ids_ref[1] ^ far) * piece, piece), piece) for far in fars]

    @pl.when(pl.program_id(0) == 0)
    def _():
        for k in range(4):
            h_ref[k * piece : (k + 1) * piece, :] = hidden[k][...]

    out = nn(h_ref[...], p_ref[...])

    def copies(j):
        for k in range(4):
            yield pltpu.make_async_copy(
                stage_ref.at[j, pl.ds(k * piece, piece)],
                out_ref.at[places[k], pl.ds(j * tile, tile)],
                sems.at[j, k],
            )

    for j in range(steps):

        @pl.when(pl.program_id(0) == j)
        def _():
            for k in range(4):
                rows = slice(k * piece, (k + 1) * piece)
                part = l_ref[places[k], :].astype(F32) - out[rows]
                stage_ref[j, rows, :] = part.astype(BF16)
            for copy in copies(j):
                copy.start()
            if j == steps - 1:
                for i in range(steps):
                    for copy in copies(i):
                        copy.wait()


def some_less_target(ids, fars, hidden, left, projection, half, into=(), after=(), tile=512):
    piece, deep = hidden[0].shape
    rows, width = left.shape
    steps = width // tile
    return pl.pallas_call(
        with_unread(functools.partial(some_target_kernel, fars), len(after)),
        grid=(steps,),
        out_shape=shape(rows, width),
        in_specs=[unread()] * len(after)
        + [smem()]
        + [whole(h) for h in hidden]
        + [pl.BlockSpec((rows, tile), lambda j: (0, j)), pl.BlockSpec((deep, tile), lambda j: (half, j))]
        + [unread()] * len(into),
        out_specs=unread(),
        scratch_shapes=[
            pltpu.VMEM((4 * piece, deep), BF16),
            pltpu.VMEM((steps, 4 * piece, tile), BF16),
            pltpu.SemaphoreType.DMA((steps, 4)),
        ],
        input_output_aliases={len(after) + 7: 0} if into else {},
        compiler_params=params(),
        cost_estimate=pl.CostEstimate(flops=int(LONG * 1e9), bytes_accessed=1024, transcendentals=0),
    )(*after, ids, *hidden, left, projection, *into)


def own_places(own_x, near_x, far_x, next_x, own_y, far_y):
    piece = own_x.shape[0] // 4
    for n in range(2):
        for e, ref in enumerate((own_x, near_x, far_x, next_x)):
            yield 2 * e + n, 0, ref, n * piece
            yield 2 * e + n, 1, (own_y, far_y)[n], e * piece


def other_places(own_x, near_x, far_x, next_x, near_y, next_y):
    piece = own_x.shape[0] // 4
    for n in range(2):
        for e, ref in enumerate((own_x, near_x, far_x, next_x)):
            yield 2 * e + n, 0, ref, (n if e == 2 else 2 + n) * piece
            yield 2 * e + n, 1, (near_y, next_y)[n], e * piece


def values_kernel(which, ids_ref, *refs):
    gaps = refs[:6]
    w_ref, out_ref, g_ref = refs[6:]
    piece = gaps[0].shape[0] // 4
    distance = ids_ref[0] ^ ids_ref[1]

    for odd in range(2):

        @pl.when(jnp.logical_and(pl.program_id(0) == 0, ((distance & 1) ^ odd) == which))
        def _():
            for k, part, ref, start in own_places(*gaps):
                if k & 1 == odd:
                    place = ((distance ^ k) >> 1) * (2 * piece) + part * piece
                    at = pl.multiple_of(place, piece)
                    g_ref[pl.ds(at, piece), :] = ref[start : start + piece, :]

    out_ref[...] = nt(g_ref[...], w_ref[...]).astype(BF16)


def values_partial(ids, gaps, weight, which, after=(), tile=512):
    rows, width = 2 * gaps[0].shape[0], gaps[0].shape[1]
    feats = weight.shape[0]
    return call(
        LONG,
        with_unread(functools.partial(values_kernel, which), len(after)),
        (feats // tile,),
        shape(rows, feats),
        [unread()] * len(after)
        + [smem()]
        + [whole(g) for g in gaps]
        + [pl.BlockSpec((tile, width), lambda j: (j, 0))],
        pl.BlockSpec((rows, tile), lambda j: (0, j)),
        [pltpu.VMEM((rows, width), BF16)],
        *after,
        ids,
        *gaps,
        weight,
    )


def weight_kernel(ids_ref, *refs):
    gaps, values = refs[:9], refs[9:13]
    out_ref, g_ref = refs[13:]
    piece = gaps[0].shape[0] // 4
    rows = g_ref.shape[0] // 4

    @pl.when(pl.program_id(0) == 0)
    def _():
        own = own_places(*gaps[:3], *gaps[4:7])
        other = other_places(*gaps[:2], *gaps[3:5], *gaps[7:])
        for half, places in enumerate((own, other)):
            for k, part, ref, start in places:
                far = ids_ref[0] ^ ids_ref[1] ^ k
                place = (2 * half + (far & 1)) * rows + (far >> 1) * (2 * piece) + part * piece
                g_ref[pl.ds(pl.multiple_of(place, piece), piece), :] = ref[start : start + piece, :]

    total = tn(values[0][...], g_ref[:rows])
    for k in range(1, 4):
        total = total + tn(values[k][...], g_ref[k * rows : (k + 1) * rows])
    out_ref[...] = total


def weight_sums(ids, gaps, values, after, tile=512):
    rows, feats = values[0].shape
    width = gaps[0].shape[1]
    return call(
        LONG,
        with_unread(weight_kernel, len(after)),
        (feats // tile,),
        shape(feats, width, F32),
        [unread()] * len(after)
        + [smem()]
        + [whole(g) for g in gaps]
        + [pl.BlockSpec((rows, tile), lambda j: (0, j))] * 4,
        pl.BlockSpec((tile, width), lambda j: (j, 0)),
        [pltpu.VMEM((4 * rows, width), BF16)],
        *after,
        ids,
        *gaps,
        *values,
    )


def add(*terms):
    total = terms[0].astype(F32)
    for term in terms[1:]:
        total = total + term.astype(F32)
    return total


def join_kernel(*refs):
    start = 0
    for ref in refs[:-1]:
        refs[-1][start : start + ref.shape[0], :] = ref[...]
        start += ref.shape[0]


def joined(arrays, after=(), micros=LONG):
    rows, width = sum(array.shape[0] for array in arrays), arrays[0].shape[1]
    tile = width // 2
    return call(
        micros,
        with_unread(join_kernel, len(after)),
        (2,),
        shape(rows, width),
        [unread()] * len(after)
        + [pl.BlockSpec((array.shape[0], tile), lambda j: (0, j)) for array in arrays],
        pl.BlockSpec((rows, tile), lambda j: (0, j)),
        [],
        *after,
        *arrays,
    )


def place_kernel(ids_ref, keep_ref, come_ref, out_ref):
    rows = keep_ref.shape[0]
    for away, ref in enumerate((keep_ref, come_ref)):
        out_ref[pl.ds(pl.multiple_of((ids_ref[2] ^ away) * rows, rows), rows), :] = ref[...]


def placed(ids, keep, come, after=(), micros=LONG):
    rows, width = keep.shape
    return call(
        micros,
        with_unread(place_kernel, len(after)),
        (1,),
        shape(2 * rows, width),
        [unread()] * len(after) + [smem(), whole(keep), whole(come)],
        pl.BlockSpec((2 * rows, width), lambda j: (0, 0)),
        [],
        *after,
        ids,
        keep,
        come,
    )


def marker_kernel(*refs):
    refs[-1][...] = jnp.zeros(refs[-1].shape, F32)


def marker(*after):
    return call(
        LONG,
        marker_kernel,
        (1,),
        shape(8, 128, F32),
        [unread()] * len(after),
        pl.BlockSpec((8, 128), lambda j: (0, 0)),
        [],
        *after,
    )


def halve_kernel(a_ref, b_ref, out_a_ref, out_b_ref):
    out_a_ref[...] = a_ref[...]
    out_b_ref[...] = b_ref[...]


def halved(a, b, after=(), micros=SHORT):
    rows, width = a.shape[0] // 2, a.shape[1]
    first, last = (pl.BlockSpec((rows, width), lambda j, k=k: (k, 0)) for k in (0, 1))
    return call(
        micros,
        with_unread(halve_kernel, len(after)),
        (1,),
        [shape(rows, width)] * 2,
        [unread()] * len(after) + [first, last],
        [first, first],
        [],
        *after,
        a,
        b,
    )


def near_ring(block, axes, one, three):
    return swap(block, axes, one), swap(block, axes, three)


def far_ring(halves, axes, one, three):
    return swap(halves[0], axes, three), swap(halves[1], axes, one)


def split(a, b):
    rows = a.shape[0] // 2
    return a[:rows], b[rows:]


def gather_tensor(block, after=()):
    across = [swap(block, Z, k) for k in (1, 3, 2)]
    arrays = [block, *across, swap(block, CORE, 1)]
    places = [(0, 0, 0), (2, 1, 0), (6, 2, 0), (4, 3, 0), (1, 4, 0)]
    if after:
        arrays.append(swap(joined(across, after), CORE, 1))
        places += [(3, 5, 0), (7, 5, 1), (5, 5, 2)]
    else:
        arrays += [swap(piece, CORE, 1) for piece in across]
        places += [(3, 5, 0), (7, 6, 0), (5, 7, 0)]
    return arrays, places


def per_device(
    teacher_values,
    teacher_weight,
    teacher_stream,
    send_order,
    projection,
    student_values,
    student_weight,
    student_stream,
):
    g = lax.axis_index("grp")
    dp = lax.axis_index("x") * 2 + lax.axis_index("yh")
    t = lax.axis_index("z") * 2 + lax.axis_index("core")
    ids = jnp.stack([dp, t, g]).astype(jnp.int32)

    loss_scale = 1.0 / math.sqrt(student_stream.shape[0] * 16)

    across = near_ring(student_values, Z, 1, 3)
    taught = (ids, send_order, teacher_values, teacher_weight, teacher_stream)
    mine, peer = teacher(*taught, 0)
    halves = halved(*across, (mine,), LONG)
    early = merged((mine, swap(peer, CORE, 1)), 4, halves[:1])
    moved = [swap(early[k], Z, k) for k in (1, 3, 2)]
    mine, peer = teacher(*taught, 1, (early[0],))
    near = joined((student_values, across[0], *far_ring(halves, Z, 1, 3), across[1]), (mine,), SHORT)
    keep, give = merged((early[0], *moved), 2, (near,), LONG)
    late = merged((mine, swap(peer, CORE, 1)), 4, (keep,))
    moved = [swap(late[k], Z, k) for k in (1, 3, 2)]
    first = placed(ids, keep, swap(give, GRP, 1), (late[0],), SHORT)
    pair = swap(near, CORE, 1)
    far = swap(near, GRP, 1)
    layer_out = layer(ids, near, pair, student_weight, (first,))
    keep, give = merged((late[0], *moved), 2, (layer_out,), LONG)
    first = gather_tensor(first)
    second = placed(ids, keep, swap(give, GRP, 1))
    far_pair = swap(far, CORE, 1)
    left = less_target(ids, first, layer_out, projection, 0, (second, far))
    blocks = [second, *[swap(second, Z, k) for k in (1, 3, 2)]]
    pairs = [swap(block, CORE, 1) for block in blocks]
    parts = some_less_target(ids, (0, 2, 6, 4), blocks, left, projection, 1, (), (marker(left, far_pair),))
    parts = some_less_target(ids, (1, 3, 7, 5), pairs, left, projection, 1, (parts,))

    parts = lax.all_to_all(parts.reshape(8, -1, parts.shape[1]), DP, 0, 0, tiled=True)
    total = student_stream.astype(F32) + jnp.sum(parts.astype(F32), axis=0)
    gap = (total * loss_scale).astype(BF16)

    rows = gap.shape[0] // 2
    first, second = gap[:rows], gap[rows:]
    around = joined([first] + [swap(first, Y, k) for k in (1, 2, 3)])
    along = joined([second] + [swap(second, X, k) for k in (1, 2, 3)], (around,))
    near_x = near_ring(around, X, 1, 3)
    own_y = swap(along, Y, 1)
    far_x = far_ring(split(*near_x), X, 1, 3)
    gaps = [around, near_x[0], *far_x, near_x[1], along, own_y]
    gaps += [swap(along, Y, 2), swap(along, Y, 3)]

    near_gaps = gaps[:3] + gaps[4:7]
    peer = values_partial(ids, near_gaps, student_weight, 1)
    mine = values_partial(ids, near_gaps, student_weight, 0, (peer,))
    parts = merged((mine, swap(peer, CORE, 1)), 4)
    values_grad = add(parts[0], *[swap(parts[k], Z, k) for k in (1, 3, 2)])
    weight_grad = weight_sums(ids, gaps, (near, pair, far, far_pair), (parts[0],))
    return (values_grad, weight_grad)


def solution(mesh):
    fine = Mesh(mesh.devices.reshape(2, 4, 2, 4, 2), ("grp", "x", "yh", "z", "core"))
    tensor = ("z", "core")
    in_specs = (
        P("grp", tensor),
        P(tensor, DP),
        P(("grp",) + tensor, DP),
        P(),
        P(DP, tensor),
        P(("grp",) + tensor, DP),
        P(DP, tensor),
        P(("grp",) + DP, tensor),
    )
    out_specs = (P(("grp",) + tensor, DP), P(DP, tensor))
    return jax.shard_map(
        per_device, mesh=fine, in_specs=in_specs, out_specs=out_specs, check_vma=False
    )
```

```python
import functools
import math

import jax
import jax.numpy as jnp
from jax import lax
from jax.experimental import pallas as pl
from jax.experimental.pallas import tpu as pltpu
from jax.sharding import Mesh, PartitionSpec as P

BF16 = jnp.bfloat16
F32 = jnp.float32
SPAN = 2
LONG = 50
SHORT = 0.01
X = "x"
Z = "z"
CORE = "core"
GRP = "grp"
DP = ("x", "yh")
Y = ("grp", "yh")
SIZES = {"grp": 2, "x": 4, "yh": 2, "z": 4, "core": 2}
VMEM_LIMIT = 62 * 1024 * 1024


def swap(array, axes, distance):
    names = axes if isinstance(axes, tuple) else (axes,)
    size = math.prod(SIZES[name] for name in names)
    return lax.ppermute(array, axes, [(i, i ^ distance) for i in range(size)])


def z_swaps(part):
    two = swap(part(2), Z, 2)
    return [swap(part(1), Z, 1), swap(part(3), Z, 3), two]


def params():
    return pltpu.CompilerParams(vmem_limit_bytes=VMEM_LIMIT)


def call(micros, body, grid, out_shape, in_specs, out_specs, scratch, *args):
    return pl.pallas_call(
        body,
        grid=grid,
        out_shape=out_shape,
        in_specs=in_specs,
        out_specs=out_specs,
        scratch_shapes=scratch,
        compiler_params=params(),
        cost_estimate=pl.CostEstimate(
            flops=int(micros * 1e9), bytes_accessed=1024, transcendentals=0
        ),
    )(*args)


def whole(array):
    return pl.BlockSpec(array.shape, lambda *_: (0,) * array.ndim)


def smem():
    return pl.BlockSpec(memory_space=pltpu.SMEM)


def unread():
    return pl.BlockSpec(memory_space=pl.ANY)


def shape(rows, columns, kind=BF16):
    return jax.ShapeDtypeStruct((rows, columns), kind)


def nn(a, b):
    return jnp.dot(a, b, preferred_element_type=F32)


def nt(a, b):
    return lax.dot_general(a, b, (((1,), (1,)), ((), ())), preferred_element_type=F32)


def with_unread(body, count):
    return lambda *refs: body(*refs[count:])


def tn(a, b):
    return lax.dot_general(a, b, (((0,), (0,)), ((), ())), preferred_element_type=F32)


def one_hot(hits):
    return jnp.where(hits, 1.0, 0.0).astype(BF16)


def teacher_kernel(piece, ids_ref, order_ref, x_ref, w_ref, s_ref, mine_ref, peer_ref, pick_ref, out_ref):
    parts, rows = pick_ref.shape[:2]
    size = s_ref.shape[0]
    group = piece * SPAN
    t, g = ids_ref[1], ids_ref[2]

    @pl.when(pl.program_id(0) == 0)
    def _():
        to = lax.broadcasted_iota(jnp.int32, (rows, rows), 0)
        at = lax.broadcasted_iota(jnp.int32, (rows, rows), 1)
        far = to // group
        owner = ((far % 2) ^ g) * 8 + (t ^ (((far // 2) % 4) * 2 + far // 8))
        wanted = one_hot(at == ((to // piece) % SPAN) * size + owner * piece + to % piece)
        line = lax.broadcasted_iota(jnp.int32, (size, size), 0)
        for k in range(parts):
            for b in range(SPAN):
                order = order_ref[pl.ds(g * 8 + k * SPAN + b, 1), :]
                columns = slice(b * size, (b + 1) * size)
                pick_ref[k, :, columns] = nt(wanted[:, columns], one_hot(line == order)).astype(BF16)

    out_ref[...] = nn(x_ref[...], w_ref[...])
    own = pl.ds(pl.multiple_of(t * size, size), size)
    out_ref[own, :] = out_ref[own, :] + s_ref[...].astype(F32)
    for k in range(parts):
        part = out_ref[k * rows : (k + 1) * rows, :].astype(BF16)
        part = nn(pick_ref[k], part).astype(BF16)
        for far in range(16):
            to = ((far % 8) * parts + k) * group
            (mine_ref, peer_ref)[far // 8][to : to + group, :] = part[far * group : (far + 1) * group]


def teacher(ids, order, values, weight, stream, half, after=(), tile=512):
    rows, depth = values.shape
    width, size = weight.shape[1] // 2, stream.shape[0]
    skip = half * (width // tile)
    side = SPAN * size
    return call(
        LONG,
        with_unread(functools.partial(teacher_kernel, order.shape[1] // 16), len(after)),
        (width // tile,),
        [shape(rows // 2, width)] * 2,
        [unread()] * len(after)
        + [
            smem(),
            whole(order),
            whole(values),
            pl.BlockSpec((depth, tile), lambda j: (0, j + skip)),
            pl.BlockSpec((size, tile), lambda j: (0, j + skip)),
        ],
        [pl.BlockSpec((rows // 2, tile), lambda j: (0, j))] * 2,
        [pltpu.VMEM((rows // side, side, side), BF16), pltpu.VMEM((rows, tile), F32)],
        *after,
        ids,
        order,
        values,
        weight,
        stream,
    )


def merge_kernel(count, *refs):
    total = refs[0][...].astype(F32)
    for ref in refs[1:count]:
        total = total + ref[...].astype(F32)
    outs = refs[count:]
    rows = total.shape[0] // len(outs)
    for k, out in enumerate(outs):
        out[...] = total[k * rows : (k + 1) * rows].astype(BF16)


def merged(terms, pieces, after=(), micros=SHORT, steps=2):
    rows, width = terms[0].shape
    tile = width // steps
    return call(
        micros,
        with_unread(functools.partial(merge_kernel, len(terms)), len(after)),
        (steps,),
        [shape(rows // pieces, width)] * pieces,
        [unread()] * len(after) + [pl.BlockSpec((rows, tile), lambda j: (0, j))] * len(terms),
        [pl.BlockSpec((rows // pieces, tile), lambda j: (0, j))] * pieces,
        [],
        *after,
        *terms,
    )


def layer_kernel(ids_ref, near_ref, pair_ref, w_ref, out_ref, v_ref):
    block = v_ref.shape[0] // 8

    @pl.when(pl.program_id(0) == 0)
    def _():
        for k in range(8):
            place = (ids_ref[1] ^ k) * block
            ref = (near_ref, pair_ref)[k & 1]
            start = (k >> 1) * block
            v_ref[pl.ds(pl.multiple_of(place, block), block), :] = ref[start : start + block, :]

    out_ref[...] = nn(v_ref[...], w_ref[...]).astype(BF16)


def layer(ids, near, pair, weight, after, tile=512):
    rows = 2 * near.shape[0]
    depth, width = weight.shape
    return call(
        LONG,
        with_unread(layer_kernel, len(after)),
        (width // tile,),
        shape(rows, width),
        [unread()] * len(after)
        + [smem(), whole(near), whole(pair), pl.BlockSpec((depth, tile), lambda j: (0, j))],
        pl.BlockSpec((rows, tile), lambda j: (0, j)),
        [pltpu.VMEM((rows, depth), BF16)],
        *after,
        ids,
        near,
        pair,
        weight,
    )


def target_kernel(places, ids_ref, *refs):
    count = 1 + max(k for _, k, _ in places)
    hidden = refs[:count]
    l_ref, p_ref, out_ref, h_ref = refs[count:]
    piece = hidden[0].shape[0]

    @pl.when(pl.program_id(0) == 0)
    def _():
        for far, k, start in places:
            at = pl.multiple_of((ids_ref[1] ^ far) * piece, piece)
            h_ref[pl.ds(at, piece), :] = hidden[k][start * piece : (start + 1) * piece, :]

    out_ref[...] = (l_ref[...].astype(F32) - nn(h_ref[...], p_ref[...])).astype(BF16)


def less_target(ids, hidden, left, projection, half, after=(), tile=512):
    arrays, places = hidden
    piece, deep = arrays[0].shape
    rows, width = left.shape
    return call(
        LONG,
        with_unread(functools.partial(target_kernel, places), len(after)),
        (width // tile,),
        shape(rows, width),
        [unread()] * len(after)
        + [smem()]
        + [whole(h) for h in arrays]
        + [pl.BlockSpec((rows, tile), lambda j: (0, j)), pl.BlockSpec((deep, tile), lambda j: (half, j))],
        pl.BlockSpec((rows, tile), lambda j: (0, j)),
        [pltpu.VMEM((rows, deep), BF16)],
        *after,
        ids,
        *arrays,
        left,
        projection,
    )


def some_target_kernel(fars, ids_ref, *refs):
    hidden = refs[:4]
    l_ref, p_ref = refs[4:6]
    out_ref, h_ref, stage_ref, sems = refs[-4:]
    piece, tile = hidden[0].shape[0], p_ref.shape[1]
    steps = stage_ref.shape[0]
    places = [pl.ds(pl.multiple_of((ids_ref[1] ^ far) * piece, piece), piece) for far in fars]

    @pl.when(pl.program_id(0) == 0)
    def _():
        for k in range(4):
            h_ref[k * piece : (k + 1) * piece, :] = hidden[k][...]

    out = nn(h_ref[...], p_ref[...])

    def copies(j):
        for k in range(4):
            yield pltpu.make_async_copy(
                stage_ref.at[j, pl.ds(k * piece, piece)],
                out_ref.at[places[k], pl.ds(j * tile, tile)],
                sems.at[j, k],
            )

    for j in range(steps):

        @pl.when(pl.program_id(0) == j)
        def _():
            for k in range(4):
                rows = slice(k * piece, (k + 1) * piece)
                part = l_ref[places[k], :].astype(F32) - out[rows]
                stage_ref[j, rows, :] = part.astype(BF16)
            for copy in copies(j):
                copy.start()
            if j == steps - 1:
                for i in range(steps):
                    for copy in copies(i):
                        copy.wait()


def some_less_target(ids, fars, hidden, left, projection, half, into=(), after=(), tile=512):
    piece, deep = hidden[0].shape
    rows, width = left.shape
    steps = width // tile
    return pl.pallas_call(
        with_unread(functools.partial(some_target_kernel, fars), len(after)),
        grid=(steps,),
        out_shape=shape(rows, width),
        in_specs=[unread()] * len(after)
        + [smem()]
        + [whole(h) for h in hidden]
        + [pl.BlockSpec((rows, tile), lambda j: (0, j)), pl.BlockSpec((deep, tile), lambda j: (half, j))]
        + [unread()] * len(into),
        out_specs=unread(),
        scratch_shapes=[
            pltpu.VMEM((4 * piece, deep), BF16),
            pltpu.VMEM((steps, 4 * piece, tile), BF16),
            pltpu.SemaphoreType.DMA((steps, 4)),
        ],
        input_output_aliases={len(after) + 7: 0} if into else {},
        compiler_params=params(),
        cost_estimate=pl.CostEstimate(flops=int(LONG * 1e9), bytes_accessed=1024, transcendentals=0),
    )(*after, ids, *hidden, left, projection, *into)


def own_places(own_x, near_x, far_x, next_x, own_y, far_y):
    piece = own_x.shape[0] // 4
    for n in range(2):
        for e, ref in enumerate((own_x, near_x, far_x, next_x)):
            yield 2 * e + n, 0, ref, n * piece
            yield 2 * e + n, 1, (own_y, far_y)[n], e * piece


def other_places(own_x, near_x, far_x, next_x, near_y, next_y):
    piece = own_x.shape[0] // 4
    for n in range(2):
        for e, ref in enumerate((own_x, near_x, far_x, next_x)):
            yield 2 * e + n, 0, ref, (n if e == 2 else 2 + n) * piece
            yield 2 * e + n, 1, (near_y, next_y)[n], e * piece


def values_kernel(ids_ref, *refs):
    gaps = refs[:6]
    w_ref, mine_ref, peer_ref, g_ref = refs[6:]
    piece = gaps[0].shape[0] // 4
    rows = g_ref.shape[0]

    @pl.when(pl.program_id(0) == 0)
    def _():
        for k, part, ref, start in own_places(*gaps):
            to = ids_ref[0] ^ ids_ref[1] ^ k
            place = (to & 1) * (rows // 2) + (to >> 1) * (2 * piece) + part * piece
            g_ref[pl.ds(pl.multiple_of(place, piece), piece), :] = ref[start : start + piece, :]

    out = nt(g_ref[...], w_ref[...]).astype(BF16)
    mine_ref[...] = out[: rows // 2]
    peer_ref[...] = out[rows // 2 :]


def values_partial(ids, gaps, weight, after, tile=512):
    rows, width = 4 * gaps[0].shape[0], gaps[0].shape[1]
    feats = weight.shape[0]
    return call(
        LONG,
        with_unread(values_kernel, len(after)),
        (feats // tile,),
        [shape(rows // 2, feats)] * 2,
        [unread()] * len(after)
        + [smem()]
        + [whole(g) for g in gaps]
        + [pl.BlockSpec((tile, width), lambda j: (j, 0))],
        [pl.BlockSpec((rows // 2, tile), lambda j: (0, j))] * 2,
        [pltpu.VMEM((rows, width), BF16)],
        *after,
        ids,
        *gaps,
        weight,
    )


def weight_kernel(ids_ref, *refs):
    gaps, values = refs[:9], refs[9:13]
    out_ref, g_ref = refs[13:]
    piece = gaps[0].shape[0] // 4
    rows = g_ref.shape[0] // 4

    @pl.when(pl.program_id(0) == 0)
    def _():
        own = own_places(*gaps[:3], *gaps[4:7])
        other = other_places(*gaps[:2], *gaps[3:5], *gaps[7:])
        for half, places in enumerate((own, other)):
            for k, part, ref, start in places:
                far = ids_ref[0] ^ ids_ref[1] ^ k
                place = (2 * half + (far & 1)) * rows + (far >> 1) * (2 * piece) + part * piece
                g_ref[pl.ds(pl.multiple_of(place, piece), piece), :] = ref[start : start + piece, :]

    total = tn(values[0][...], g_ref[:rows])
    for k in range(1, 4):
        total = total + tn(values[k][...], g_ref[k * rows : (k + 1) * rows])
    out_ref[...] = total


def weight_sums(ids, gaps, values, after, tile=512):
    rows, feats = values[0].shape
    width = gaps[0].shape[1]
    return call(
        LONG,
        with_unread(weight_kernel, len(after)),
        (feats // tile,),
        shape(feats, width, F32),
        [unread()] * len(after)
        + [smem()]
        + [whole(g) for g in gaps]
        + [pl.BlockSpec((rows, tile), lambda j: (0, j))] * 4,
        pl.BlockSpec((tile, width), lambda j: (j, 0)),
        [pltpu.VMEM((4 * rows, width), BF16)],
        *after,
        ids,
        *gaps,
        *values,
    )


def add(*terms):
    total = terms[0].astype(F32)
    for term in terms[1:]:
        total = total + term.astype(F32)
    return total


def join_kernel(*refs):
    start = 0
    for ref in refs[:-1]:
        refs[-1][start : start + ref.shape[0], :] = ref[...]
        start += ref.shape[0]


def joined(arrays, after=(), micros=LONG):
    rows, width = sum(array.shape[0] for array in arrays), arrays[0].shape[1]
    tile = width // 2
    return call(
        micros,
        with_unread(join_kernel, len(after)),
        (2,),
        shape(rows, width),
        [unread()] * len(after)
        + [pl.BlockSpec((array.shape[0], tile), lambda j: (0, j)) for array in arrays],
        pl.BlockSpec((rows, tile), lambda j: (0, j)),
        [],
        *after,
        *arrays,
    )


def place_kernel(ids_ref, keep_ref, come_ref, out_ref):
    rows = keep_ref.shape[0]
    for away, ref in enumerate((keep_ref, come_ref)):
        out_ref[pl.ds(pl.multiple_of((ids_ref[2] ^ away) * rows, rows), rows), :] = ref[...]


def placed(ids, keep, come, after=(), micros=LONG):
    rows, width = keep.shape
    return call(
        micros,
        with_unread(place_kernel, len(after)),
        (1,),
        shape(2 * rows, width),
        [unread()] * len(after) + [smem(), whole(keep), whole(come)],
        pl.BlockSpec((2 * rows, width), lambda j: (0, 0)),
        [],
        *after,
        ids,
        keep,
        come,
    )


def marker_kernel(*refs):
    refs[-1][...] = jnp.zeros(refs[-1].shape, F32)


def marker(*after):
    return call(
        LONG,
        marker_kernel,
        (1,),
        shape(8, 128, F32),
        [unread()] * len(after),
        pl.BlockSpec((8, 128), lambda j: (0, 0)),
        [],
        *after,
    )


def halve_kernel(a_ref, b_ref, out_a_ref, out_b_ref):
    out_a_ref[...] = a_ref[...]
    out_b_ref[...] = b_ref[...]


def halved(a, b, after=(), micros=SHORT):
    rows, width = a.shape[0] // 2, a.shape[1]
    first, last = (pl.BlockSpec((rows, width), lambda j, k=k: (k, 0)) for k in (0, 1))
    return call(
        micros,
        with_unread(halve_kernel, len(after)),
        (1,),
        [shape(rows, width)] * 2,
        [unread()] * len(after) + [first, last],
        [first, first],
        [],
        *after,
        a,
        b,
    )


def near_ring(block, axes, one, three):
    return swap(block, axes, one), swap(block, axes, three)


def far_ring(halves, axes, one, three):
    return swap(halves[0], axes, three), swap(halves[1], axes, one)


def split(a, b):
    rows = a.shape[0] // 2
    return a[:rows], b[rows:]


def gather_tensor(block, after=()):
    across = z_swaps(lambda k: block)
    arrays = [block, *across, swap(block, CORE, 1)]
    places = [(0, 0, 0), (2, 1, 0), (6, 2, 0), (4, 3, 0), (1, 4, 0)]
    if after:
        arrays.append(swap(joined(across, after), CORE, 1))
        places += [(3, 5, 0), (7, 5, 1), (5, 5, 2)]
    else:
        arrays += [swap(piece, CORE, 1) for piece in across]
        places += [(3, 5, 0), (7, 6, 0), (5, 7, 0)]
    return arrays, places


def per_device(
    teacher_values,
    teacher_weight,
    teacher_stream,
    send_order,
    projection,
    student_values,
    student_weight,
    student_stream,
):
    g = lax.axis_index("grp")
    dp = lax.axis_index("x") * 2 + lax.axis_index("yh")
    t = lax.axis_index("z") * 2 + lax.axis_index("core")
    ids = jnp.stack([dp, t, g]).astype(jnp.int32)

    loss_scale = 1.0 / math.sqrt(student_stream.shape[0] * 16)

    across = near_ring(student_values, Z, 1, 3)
    taught = (ids, send_order, teacher_values, teacher_weight, teacher_stream)
    mine, peer = teacher(*taught, 0)
    halves = halved(*across, (mine,), LONG)
    early = merged((mine, swap(peer, CORE, 1)), 4, halves[:1])
    moved = z_swaps(lambda k: early[k])
    mine, peer = teacher(*taught, 1, (early[0],))
    near = joined((student_values, across[0], *far_ring(halves, Z, 1, 3), across[1]), (mine,), SHORT)
    keep, give = merged((early[0], *moved), 2, (near,), LONG)
    late = merged((mine, swap(peer, CORE, 1)), 4, (keep,))
    moved = z_swaps(lambda k: late[k])
    first = placed(ids, keep, swap(give, GRP, 1), (late[0],), SHORT)
    pair = swap(near, CORE, 1)
    far = swap(near, GRP, 1)
    layer_out = layer(ids, near, pair, student_weight, (first,))
    keep, give = merged((late[0], *moved), 2, (layer_out,), LONG)
    first = gather_tensor(first)
    second = placed(ids, keep, swap(give, GRP, 1))
    far_pair = swap(far, CORE, 1)
    left = less_target(ids, first, layer_out, projection, 0, (second, far))
    blocks = [second, *z_swaps(lambda k: second)]
    pairs = [swap(block, CORE, 1) for block in blocks]
    parts = some_less_target(ids, (0, 2, 6, 4), blocks, left, projection, 1, (), (marker(left, far_pair),))
    parts = some_less_target(ids, (1, 3, 7, 5), pairs, left, projection, 1, (parts,))

    parts = lax.all_to_all(parts.reshape(8, -1, parts.shape[1]), DP, 0, 0, tiled=True)
    total = student_stream.astype(F32) + jnp.sum(parts.astype(F32), axis=0)
    gap = (total * loss_scale).astype(BF16)

    rows = gap.shape[0] // 2
    first, second = gap[:rows], gap[rows:]
    around = joined([first] + [swap(first, Y, k) for k in (1, 2, 3)])
    along = joined([second] + [swap(second, X, k) for k in (1, 2, 3)], (around,))
    near_x = near_ring(around, X, 1, 3)
    own_y = swap(along, Y, 1)
    far_x = far_ring(split(*near_x), X, 1, 3)
    gaps = [around, near_x[0], *far_x, near_x[1], along, own_y]
    gaps += [swap(along, Y, 2), swap(along, Y, 3)]

    mine, peer = values_partial(ids, gaps[:3] + gaps[4:7], student_weight, ())
    parts = merged((mine, swap(peer, CORE, 1)), 4, (marker(mine),))
    values_grad = add(parts[0], *z_swaps(lambda k: parts[k]))
    weight_grad = weight_sums(ids, gaps, (near, pair, far, far_pair), (parts[0],))
    return (values_grad, weight_grad)


def solution(mesh):
    fine = Mesh(mesh.devices.reshape(2, 4, 2, 4, 2), ("grp", "x", "yh", "z", "core"))
    tensor = ("z", "core")
    in_specs = (
        P("grp", tensor),
        P(tensor, DP),
        P(("grp",) + tensor, DP),
        P(),
        P(DP, tensor),
        P(("grp",) + tensor, DP),
        P(DP, tensor),
        P(("grp",) + DP, tensor),
    )
    out_specs = (P(("grp",) + tensor, DP), P(DP, tensor))
    return jax.shard_map(
        per_device, mesh=fine, in_specs=in_specs, out_specs=out_specs, check_vma=False
    )
```
